32 devices in a mesh: member: 4 (over z), token: 8 (over y, x, core).
Axes of the slice: x: 2, y: 2, z: 4, core: 2. Of those that a mesh axis runs over, the one named last changes fastest.
Arguments:
- members_in: bfloat16 [8, 1024, 1024], P('member', 'token'), may hold values from -6 to 6
- member_noise: bfloat16 [8, 1024, 1024], P('member', 'token'), may hold values from -6 to 6
- norm_gain: float32 [1024], replicated, may hold values from 0.25 to 1.75
- weight_query: bfloat16 [1024, 1024], replicated, may hold values from -0.1875 to 0.1875
- weight_key: bfloat16 [1024, 1024], replicated, may hold values from -0.1875 to 0.1875
- weight_value: bfloat16 [1024, 1024], replicated, may hold values from -0.1875 to 0.1875
- weight_out: bfloat16 [1024, 1024], replicated, may hold values from -0.1875 to 0.1875
- decoder_projection_weight: bfloat16 [100, 1024], replicated, may hold values from -0.1875 to 0.1875
- decoder_bias: float32 [100], replicated, may hold values from -3 to 3
- observations: float32 [100, 8192], P(None, 'token'), may hold values from -6 to 6
- surface_extent_factor: float32 [8192], P('token'), may hold values from 0.3 to 3
- quantity_scoring_factor: float32 [100], replicated, may hold values from 0.2 to 2
- point_map: int32 [8192], P('token'), may hold values from 0 to 127
Outputs:
- mean_scoring: float32 [], replicated
- grad_members: bfloat16 [8, 1024, 1024], P('member', 'token')
- grad_out: float32 [1024, 1024], P('token')
- grad_decoder: float32 [100, 1024], replicated
The draws below stay inside these ranges and needn't reach their ends.
Inputs may be any that keep to these rules, and one draw needn't show every extreme that they name: Point p belongs to token (p // 1024) * 128 + point_map[p].
All inputs are finite; a program needn't handle non-finite values.
Results may differ from the reference program's by a relative error of at most 0.015.
Values may be sent and summed in bfloat16 or wider, within the bound.
A program may use at most 128 MiB of HBM per device.

```python
import math
import jax
import jax.numpy as jnp
from jax import lax

HEADS = 16
VARS = 100
HALF = 128
TOK_DEV = 128
C = 1024
SITES_EACH_PART = 1024
MEMBERS = 8
TOKENS = 1024
POINTS = 8192


def set_ends(values, key, least, top_value):
    place = [jax.random.randint(jax.random.fold_in(key, axis), (), 0, length) for axis, length in enumerate(values.shape)]
    main_axis = values.shape.index(max(values.shape))
    next_to = place[:main_axis] + [(place[main_axis] + 1) % values.shape[main_axis]] + place[main_axis + 1:]
    return values.at[tuple(place)].set(least).at[tuple(next_to)].set(top_value)


def with_spikes(result, rng, source, target, shards_of, factor):
    owner, partner = [(jnp.arange(result.shape[position]) // (result.shape[position] // shards_of)).reshape([-1 if axis == position else 1 for axis in range(result.ndim)]) for position in (source, target)]
    chosen = jax.random.permutation(rng, shards_of)[partner]
    strong = (owner == chosen) | (owner == (partner + shards_of // 2) % shards_of)
    return jnp.where(strong, factor * result, result)


def steps_of(stream_key, dims, shards, least, top_value):
    def one(position, blocks):
        heights = jax.random.uniform(jax.random.fold_in(jax.random.fold_in(stream_key, 6), position), (blocks,), jnp.float32, least / len(shards), top_value / len(shards))
        return jnp.repeat(jnp.exp(heights), dims[position] // blocks).reshape((-1,) + (1,) * (len(dims) - position - 1))

    level = one(*shards[0])
    for cut in shards[1:]:
        level = level * one(*cut)
    return level


def gaussian(stream_key, shape, scale, most, cuts=(), kind=jnp.bfloat16):
    entries = jax.random.normal(stream_key, shape, jnp.float32) * scale
    if len(cuts) > 0:
        entries = steps_of(stream_key, shape, cuts, -0.22, 0.18) * entries
    return jnp.clip(entries, min=-most, max=most).astype(kind)


def gaussian_with(rng, dims, deviation, most, shards, heavy, held_as=jnp.bfloat16):
    values = deviation * jax.random.normal(rng, dims, jnp.float32)
    if shards:
        values = values * steps_of(rng, dims, shards, -0.22, 0.18)
    return jnp.clip(with_spikes(values, jax.random.fold_in(rng, 3), *heavy), -most, most).astype(held_as)


def setup_inputs(seed: int = 0) -> dict:
    key_list = jax.random.split(jax.random.key(seed), 14)
    return {
        "members_in": gaussian_with(key_list[0], (MEMBERS, TOKENS, C), 1.0, 6.0, ((0, 4), (1, 8)), (1, 2, 8, 2.0)),
        "member_noise": gaussian(key_list[1], (MEMBERS, TOKENS, C), 1.0, 6.0, ((0, 4), (1, 8))),
        "norm_gain": jnp.clip(1.0 + 0.15 * jax.random.normal(key_list[2], (C,), jnp.float32), 0.25, 1.75),
        "weight_query": gaussian(key_list[3], (C, C), C ** -0.5, 0.1875),
        "weight_key": gaussian(key_list[4], (C, C), C ** -0.5, 0.1875),
        "weight_value": gaussian(key_list[5], (C, C), C ** -0.5, 0.1875),
        "weight_out": gaussian(key_list[6], (C, C), C ** -0.5, 0.1875),
        "decoder_projection_weight": gaussian(key_list[7], (VARS, C), C ** -0.5, 0.1875),
        "decoder_bias": gaussian(key_list[8], (VARS,), 0.5, 3.0, (), jnp.float32),
        "observations": gaussian(key_list[9], (VARS, POINTS), 1.0, 6.0, ((1, 8),), jnp.float32),
        "surface_extent_factor": jnp.clip(jnp.exp(math.log(3.0) - 2.3025851 * jax.random.uniform(key_list[10], (POINTS,), jnp.float32) ** steps_of(key_list[10], (POINTS,), ((0, 8),), -0.2, 0.2)), 0.3, 3.0),
        "quantity_scoring_factor": jnp.clip(jnp.exp(jax.random.uniform(key_list[11], (VARS,), jnp.float32, math.log(0.2), math.log(2.0))), 0.2, 2.0),
        "point_map": set_ends(jax.random.randint(key_list[12], (POINTS,), 0, TOK_DEV), jax.random.fold_in(key_list[12], 1), 0, TOK_DEV - 1).astype(jnp.int32),
    }


EPSILON = 1e-06
SMOOTH = 0.01

def normalize_heads(flat):
    rows, width = flat.shape
    split = flat.reshape(rows, HEADS, width // HEADS)
    split = split * lax.rsqrt(lax.optimization_barrier(jnp.mean(split * split, axis=-1, keepdims=True)) + EPSILON)
    return split.reshape(rows, width)

def project(state_in, member_noise, norm_gain, weight_query, weight_key, weight_value):
    member_rows, tokens, width = state_in.shape
    mixed = state_in + member_noise.astype(jnp.float32)
    normed = (mixed * lax.rsqrt(lax.optimization_barrier(jnp.mean(mixed * mixed, axis=-1, keepdims=True)) + EPSILON) * norm_gain).astype(jnp.bfloat16)
    flat = normed.reshape(member_rows * tokens, width)
    query = normalize_heads(jnp.dot(flat, weight_query, preferred_element_type=jnp.float32)).astype(jnp.bfloat16)
    key = normalize_heads(jnp.dot(flat, weight_key, preferred_element_type=jnp.float32)).astype(jnp.bfloat16)
    value = jnp.dot(flat, weight_value, preferred_element_type=jnp.float32).astype(jnp.bfloat16)
    full_shape = (member_rows, tokens, width)
    return (query.reshape(full_shape), key.reshape(full_shape), value.reshape(full_shape))

def attend(query, keys, values, leading_realization, total):
    member_rows, queries, width = query.shape
    realization_number = keys.shape[1]
    depth = width // HEADS
    query_heads = query.reshape(member_rows, queries, HEADS, depth).astype(jnp.float32)
    key_heads = keys.reshape(member_rows, realization_number, HEADS, depth).astype(jnp.float32)
    value_heads = values.reshape(member_rows, realization_number, HEADS, depth).astype(jnp.float32)
    scores = jnp.einsum('mqhd,mkhd->mhqk', query_heads, key_heads) / jnp.sqrt(jnp.float32(depth))
    query_pos = leading_realization + lax.iota(jnp.int32, queries)
    key_pos = leading_realization - HALF + lax.iota(jnp.int32, realization_number)
    allowed = (key_pos[None, :] >= query_pos[:, None] - HALF) & (key_pos[None, :] < query_pos[:, None] + HALF)
    allowed = allowed & (key_pos[None, :] >= 0) & (key_pos[None, :] < total)
    raised = jnp.where(allowed[None, None], jnp.exp(scores), jnp.float32(0.0))
    probs = (raised / lax.optimization_barrier(jnp.sum(raised, axis=-1, keepdims=True))).astype(jnp.bfloat16)
    mixed = jnp.einsum('mhqk,mkhd->mqhd', probs.astype(jnp.float32), value_heads)
    return mixed.reshape(member_rows, queries, width).astype(jnp.bfloat16)

def windowed(query, key, value):
    member_rows, total, width = query.shape
    padding = ((0, 0), (HALF, HALF), (0, 0))
    key_pad = jnp.pad(key, padding)
    value_pad = jnp.pad(value, padding)

    def block(index):
        beginning_shift = index * TOK_DEV
        query_block = lax.dynamic_slice_in_dim(query, beginning_shift, TOK_DEV, 1)
        key_block = lax.dynamic_slice_in_dim(key_pad, beginning_shift, TOK_DEV + 2 * HALF, 1)
        value_block = lax.dynamic_slice_in_dim(value_pad, beginning_shift, TOK_DEV + 2 * HALF, 1)
        return attend(query_block, key_block, value_block, beginning_shift, total)
    stacked = lax.map(jax.checkpoint(block), jnp.arange(total // TOK_DEV, dtype=jnp.int32))
    return jnp.transpose(stacked, (1, 0, 2, 3)).reshape(member_rows, total, width)

def softened_magnitude(diff):
    return jnp.sqrt(diff * diff + SMOOTH)

def unbiased_ranked_score(realization_prediction, observed_grid, surface_extent, quantity_scoring_factor):
    realization_number = realization_prediction.shape[0]
    accuracy_part = softened_magnitude(realization_prediction[0] - observed_grid)
    for realization_position in range(1, realization_number):
        accuracy_part = accuracy_part + softened_magnitude(realization_prediction[realization_position] - observed_grid)
    dispersion_part = jnp.zeros_like(accuracy_part)
    for leading_realization in range(realization_number):
        for paired_realization in range(leading_realization + 1, realization_number):
            dispersion_part = dispersion_part + softened_magnitude(realization_prediction[leading_realization] - realization_prediction[paired_realization])
    score = accuracy_part / realization_number - dispersion_part / (realization_number * (realization_number - 1))
    return jnp.sum(quantity_scoring_factor[:, None] * surface_extent[None, :] * score)

def reference(members_in, member_noise, norm_gain, weight_query, weight_key, weight_value, weight_out, decoder_projection_weight, decoder_bias, observations, surface_extent_factor, quantity_scoring_factor, point_map):
    location_entry_position = jnp.arange(POINTS, dtype=jnp.int32) // SITES_EACH_PART * TOK_DEV + point_map

    def overall_scoring_amount(state, out_f, decoder_f):
        member_rows, tokens, width = state.shape
        query, key, value = project(state, member_noise, norm_gain, weight_query, weight_key, weight_value)
        attended = windowed(query, key, value)
        update = jnp.dot(attended.reshape(member_rows * tokens, width), out_f.astype(jnp.bfloat16), preferred_element_type=jnp.float32)
        residual_stream_state = (state + member_noise.astype(jnp.float32) + update.reshape(member_rows, tokens, width)).astype(jnp.bfloat16)
        mapping_array = jnp.einsum('vc,mtc->mvt', decoder_f.astype(jnp.bfloat16).astype(jnp.float32), residual_stream_state.astype(jnp.float32))
        mapping_array = mapping_array + decoder_bias[None, :, None]
        realization_prediction = jnp.take(mapping_array, location_entry_position, axis=2)

        def block(index):
            beginning_shift = index * SITES_EACH_PART
            return unbiased_ranked_score(lax.dynamic_slice_in_dim(realization_prediction, beginning_shift, SITES_EACH_PART, 2), lax.dynamic_slice_in_dim(observations, beginning_shift, SITES_EACH_PART, 1), lax.dynamic_slice_in_dim(surface_extent_factor, beginning_shift, SITES_EACH_PART, 0), quantity_scoring_factor)
        parts = lax.map(jax.checkpoint(block), jnp.arange(POINTS // SITES_EACH_PART, dtype=jnp.int32))
        return jnp.sum(parts)
    total, pull = jax.vjp(overall_scoring_amount, members_in.astype(jnp.float32), weight_out.astype(jnp.float32), decoder_projection_weight.astype(jnp.float32))
    grad_state, grad_out, grad_decoder = pull(jnp.ones((), jnp.float32))
    mean_scoring = total / (VARS * POINTS)
    return (mean_scoring, grad_state.astype(jnp.bfloat16), grad_out, grad_decoder)
```

```python
import jax
import jax.numpy as jnp
from jax import lax
from jax.sharding import PartitionSpec as P

HEADS = 16
HALF = 128


EPSILON = 1e-06
SMOOTH = 0.01


def extended_2(block, sides, width):
    for axis, dim in sides:
        count = lax.axis_size(axis)
        forward = [(i, i + 1) for i in range(count - 1)]
        backward = [(target, source) for source, target in forward]
        low = lax.ppermute(
            lax.slice_in_dim(block, block.shape[dim] - width, None, axis=dim), axis, forward
        )
        high = lax.ppermute(lax.slice_in_dim(block, 0, width, axis=dim), axis, backward)
        block = jnp.concatenate([low, block, high], axis=dim)
    return block


def from_behind(block, axis, distance):
    devices = range(lax.axis_size(axis))
    route = [(i - distance, i) for i in devices if i - distance in devices]
    return lax.ppermute(block, axis, route)


def normalize_heads(flat):
    rows, width = flat.shape
    split = flat.reshape(rows, HEADS, width // HEADS)
    split = split * lax.rsqrt(jnp.mean(split * split, axis=-1, keepdims=True) + EPSILON)
    return split.reshape(rows, width)


def project(state_in, member_noise, norm_gain, weight_query, weight_key, weight_value):
    member_rows, tokens, width = state_in.shape
    mixed = state_in + member_noise.astype(jnp.float32)
    normed = (
        mixed * lax.rsqrt(jnp.mean(mixed * mixed, axis=-1, keepdims=True) + EPSILON) * norm_gain
    ).astype(jnp.bfloat16)
    flat = normed.reshape(member_rows * tokens, width)
    query = normalize_heads(jnp.dot(flat, weight_query, preferred_element_type=jnp.float32)).astype(
        jnp.bfloat16
    )
    key = normalize_heads(jnp.dot(flat, weight_key, preferred_element_type=jnp.float32)).astype(
        jnp.bfloat16
    )
    value = jnp.dot(flat, weight_value, preferred_element_type=jnp.float32).astype(jnp.bfloat16)
    full_shape = (member_rows, tokens, width)
    return (query.reshape(full_shape), key.reshape(full_shape), value.reshape(full_shape))


def attend(query, keys, values, leading_realization, total):
    member_rows, queries, width = query.shape
    realization_number = keys.shape[1]
    depth = width // HEADS
    query_heads = query.reshape(member_rows, queries, HEADS, depth)
    key_heads = keys.reshape(member_rows, realization_number, HEADS, depth)
    value_heads = values.reshape(member_rows, realization_number, HEADS, depth)
    scores = jnp.einsum(
        "mqhd,mkhd->mhqk", query_heads, key_heads, preferred_element_type=jnp.float32
    ) / jnp.sqrt(jnp.float32(depth))
    query_pos = leading_realization + lax.iota(jnp.int32, queries)
    key_pos = leading_realization - HALF + lax.iota(jnp.int32, realization_number)
    allowed = (key_pos[None, :] >= query_pos[:, None] - HALF) & (
        key_pos[None, :] < query_pos[:, None] + HALF
    )
    allowed = allowed & (key_pos[None, :] >= 0) & (key_pos[None, :] < total)
    raised = jnp.where(allowed[None, None], jnp.exp(scores), jnp.float32(0.0))
    probs = (raised / jnp.sum(raised, axis=-1, keepdims=True)).astype(jnp.bfloat16)
    mixed = jnp.einsum("mhqk,mkhd->mqhd", probs, value_heads, preferred_element_type=jnp.float32)
    return mixed.reshape(member_rows, queries, width).astype(jnp.bfloat16)


def split_product(left, right, equation):
    high = left.astype(jnp.bfloat16)
    low = (left - high.astype(jnp.float32)).astype(jnp.bfloat16)
    first = jnp.einsum(equation, high, right, preferred_element_type=jnp.float32)
    return first + jnp.einsum(equation, low, right, preferred_element_type=jnp.float32)


def score_and_slope(own, observed, surface_extent, quantity, point_map):
    member_rows, _, tokens = own.shape
    onehot = point_map[:, None] == lax.iota(jnp.int32, tokens)[None, :]
    token_area = jnp.sum(jnp.where(onehot, surface_extent[:, None], 0.0), axis=0)
    onehot = onehot.astype(jnp.bfloat16)
    everyone = lax.all_gather(own, "member", axis=0, tiled=True)
    count = everyone.shape[0]
    diff = split_product(own, onehot, "mvt,pt->mvp") - observed[None]
    inverse = lax.rsqrt(diff * diff + SMOOTH)
    weight = quantity[:, None] * surface_extent[None, :] / count
    weighted = weight[None] * inverse
    share = jnp.sum(weighted * (diff * diff + SMOOTH))
    slope = split_product(weighted * diff, onehot, "mvp,pt->mvt")
    first = lax.axis_index("member") * member_rows
    pair_weight = quantity[:, None] * token_area[None, :] / (count * (count - 1))
    for row in range(member_rows):
        magnitude = jnp.zeros_like(own[0])
        pulled = jnp.zeros_like(own[0])
        for other in range(count):
            gap = own[row] - everyone[other]
            square = gap * gap + SMOOTH
            upside = lax.rsqrt(square)
            keep = jnp.where(first + row == other, 0.0, 0.5)
            magnitude = magnitude + keep * square * upside
            pulled = pulled + gap * upside
        share = share - jnp.sum(pair_weight * magnitude)
        slope = slope.at[row].add(-pair_weight * pulled)
    return share, slope


def shards(
    members_in,
    member_noise,
    norm_gain,
    weight_query,
    weight_key,
    weight_value,
    weight_out,
    decoder_projection_weight,
    decoder_bias,
    observations,
    surface_extent_factor,
    quantity_scoring_factor,
    point_map,
):
    member_rows, tokens, width = members_in.shape
    state = members_in.astype(jnp.float32)

    def front(state_in):
        return project(state_in, member_noise, norm_gain, weight_query, weight_key, weight_value)

    (query, key, value), front_pull = jax.vjp(front, state)
    stacked = jnp.stack([key, value])
    extended = extended_2(stacked, (("token", 2),), HALF)
    leading_realization = lax.axis_index("token") * tokens
    total = tokens * lax.axis_size("token")

    def middle(query_in, extended_in):
        return attend(query_in, extended_in[0], extended_in[1], leading_realization, total)

    attended, middle_pull = jax.vjp(middle, query, extended)
    flat_att = attended.reshape(member_rows * tokens, width)
    update = jnp.dot(flat_att, weight_out, preferred_element_type=jnp.float32).reshape(
        member_rows, tokens, width
    )
    residual_stream_state = (state + member_noise.astype(jnp.float32) + update).astype(jnp.bfloat16)

    own = jnp.einsum(
        "vc,mtc->mvt",
        decoder_projection_weight,
        residual_stream_state,
        preferred_element_type=jnp.float32,
    )
    own = own + decoder_bias[None, :, None]
    share, slope = score_and_slope(
        own, observations, surface_extent_factor, quantity_scoring_factor, point_map
    )
    slope = slope.astype(jnp.bfloat16)
    decoder_piece = jnp.einsum(
        "mvt,mtc->vc", slope, residual_stream_state, preferred_element_type=jnp.float32
    )
    carried_slope = jnp.einsum(
        "mvt,vc->mtc", slope, decoder_projection_weight, preferred_element_type=jnp.float32
    ).astype(jnp.bfloat16)
    overall_scoring_amount, grad_decoder = lax.psum((share, decoder_piece), ("member", "token"))
    mean_scoring = overall_scoring_amount / (
        observations.shape[0] * observations.shape[1] * lax.axis_size("token")
    )
    flat_grad = carried_slope.reshape(member_rows * tokens, width)
    grad_attended = (
        jnp.dot(flat_grad, weight_out.T, preferred_element_type=jnp.float32)
        .astype(jnp.bfloat16)
        .reshape(member_rows, tokens, width)
    )
    grad_query, grad_extended = middle_pull(grad_attended)
    lower_rim = grad_extended[:, :, :HALF]
    upper_rim = grad_extended[:, :, tokens + HALF :]
    inner = grad_extended[:, :, HALF : tokens + HALF].astype(jnp.float32)
    from_next = from_behind(lower_rim, "token", -1)
    from_prev = from_behind(upper_rim, "token", 1)
    inner = inner.at[:, :, tokens - HALF :].add(from_next.astype(jnp.float32))
    inner = inner.at[:, :, :HALF].add(from_prev.astype(jnp.float32))
    (grad_front,) = front_pull(
        (grad_query, inner[0].astype(jnp.bfloat16), inner[1].astype(jnp.bfloat16))
    )
    grad_members = (grad_front + carried_slope.astype(jnp.float32)).astype(jnp.bfloat16)
    contract = (((0,), (0,)), ((), ()))
    product = lax.dot_general(flat_att, flat_grad, contract, preferred_element_type=jnp.float32)
    scattered = lax.psum_scatter(
        product.astype(jnp.bfloat16), "token", scatter_dimension=0, tiled=True
    )
    grad_out = lax.psum(scattered.astype(jnp.float32), "member")
    return (mean_scoring, grad_members, grad_out, grad_decoder)


def solution(mesh):
    return jax.shard_map(
        shards,
        mesh=mesh,
        in_specs=(
            P("member", "token", None),
            P("member", "token", None),
            P(),
            P(),
            P(),
            P(),
            P(),
            P(),
            P(),
            P(None, "token"),
            P("token"),
            P(),
            P("token"),
        ),
        out_specs=(P(), P("member", "token", None), P("token", None), P()),
        check_vma=False,
    )
```

```python
import functools

import jax
import jax.numpy as jnp
from jax import lax
from jax.experimental import pallas as pl
from jax.experimental.pallas import tpu as pltpu
from jax.sharding import PartitionSpec as P

HEADS = 16
HALF = 128


EPSILON = 1e-06
SMOOTH = 0.01


def extended_2(block, sides, width):
    for axis, dim in sides:
        count = lax.axis_size(axis)
        forward = [(i, i + 1) for i in range(count - 1)]
        backward = [(target, source) for source, target in forward]
        low = lax.ppermute(
            lax.slice_in_dim(block, block.shape[dim] - width, None, axis=dim), axis, forward
        )
        high = lax.ppermute(lax.slice_in_dim(block, 0, width, axis=dim), axis, backward)
        block = jnp.concatenate([low, block, high], axis=dim)
    return block


def from_behind(block, axis, distance):
    devices = range(lax.axis_size(axis))
    route = [(i - distance, i) for i in devices if i - distance in devices]
    return lax.ppermute(block, axis, route)


def normalize_heads(flat):
    rows, width = flat.shape
    split = flat.reshape(rows, HEADS, width // HEADS)
    split = split * lax.rsqrt(jnp.mean(split * split, axis=-1, keepdims=True) + EPSILON)
    return split.reshape(rows, width)


def project(state_in, member_noise, norm_gain, weight_query, weight_key, weight_value):
    member_rows, tokens, width = state_in.shape
    mixed = state_in + member_noise.astype(jnp.float32)
    normed = (
        mixed * lax.rsqrt(jnp.mean(mixed * mixed, axis=-1, keepdims=True) + EPSILON) * norm_gain
    ).astype(jnp.bfloat16)
    flat = normed.reshape(member_rows * tokens, width)
    query = normalize_heads(jnp.dot(flat, weight_query, preferred_element_type=jnp.float32)).astype(
        jnp.bfloat16
    )
    key = normalize_heads(jnp.dot(flat, weight_key, preferred_element_type=jnp.float32)).astype(
        jnp.bfloat16
    )
    value = jnp.dot(flat, weight_value, preferred_element_type=jnp.float32).astype(jnp.bfloat16)
    full_shape = (member_rows, tokens, width)
    return (query.reshape(full_shape), key.reshape(full_shape), value.reshape(full_shape))


def attend(query, keys, values, leading_realization, total):
    member_rows, queries, width = query.shape
    realization_number = keys.shape[1]
    depth = width // HEADS
    query_heads = query.reshape(member_rows, queries, HEADS, depth)
    key_heads = keys.reshape(member_rows, realization_number, HEADS, depth)
    value_heads = values.reshape(member_rows, realization_number, HEADS, depth)
    scores = jnp.einsum(
        "mqhd,mkhd->mhqk", query_heads, key_heads, preferred_element_type=jnp.float32
    ) / jnp.sqrt(jnp.float32(depth))
    query_pos = leading_realization + lax.iota(jnp.int32, queries)
    key_pos = leading_realization - HALF + lax.iota(jnp.int32, realization_number)
    allowed = (key_pos[None, :] >= query_pos[:, None] - HALF) & (
        key_pos[None, :] < query_pos[:, None] + HALF
    )
    allowed = allowed & (key_pos[None, :] >= 0) & (key_pos[None, :] < total)
    raised = jnp.where(allowed[None, None], jnp.exp(scores), jnp.float32(0.0))
    probs = (raised / jnp.sum(raised, axis=-1, keepdims=True)).astype(jnp.bfloat16)
    mixed = jnp.einsum("mhqk,mkhd->mqhd", probs, value_heads, preferred_element_type=jnp.float32)
    return mixed.reshape(member_rows, queries, width).astype(jnp.bfloat16)


def split_product(left, right, equation):
    high = left.astype(jnp.bfloat16)
    low = (left - high.astype(jnp.float32)).astype(jnp.bfloat16)
    first = jnp.einsum(equation, high, right, preferred_element_type=jnp.float32)
    return first + jnp.einsum(equation, low, right, preferred_element_type=jnp.float32)


def score_and_slope(own, observed, surface_extent, quantity, point_map):
    member_rows, _, tokens = own.shape
    onehot = point_map[:, None] == lax.iota(jnp.int32, tokens)[None, :]
    token_area = jnp.sum(jnp.where(onehot, surface_extent[:, None], 0.0), axis=0)
    onehot = onehot.astype(jnp.bfloat16)
    everyone = lax.all_gather(own, "member", axis=0, tiled=True)
    count = everyone.shape[0]
    diff = split_product(own, onehot, "mvt,pt->mvp") - observed[None]
    inverse = lax.rsqrt(diff * diff + SMOOTH)
    weight = quantity[:, None] * surface_extent[None, :] / count
    weighted = weight[None] * inverse
    share = jnp.sum(weighted * (diff * diff + SMOOTH))
    slope = split_product(weighted * diff, onehot, "mvp,pt->mvt")
    first = lax.axis_index("member") * member_rows
    pair_weight = quantity[:, None] * token_area[None, :] / (count * (count - 1))
    for row in range(member_rows):
        magnitude = jnp.zeros_like(own[0])
        pulled = jnp.zeros_like(own[0])
        for other in range(count):
            gap = own[row] - everyone[other]
            square = gap * gap + SMOOTH
            upside = lax.rsqrt(square)
            keep = jnp.where(first + row == other, 0.0, 0.5)
            magnitude = magnitude + keep * square * upside
            pulled = pulled + gap * upside
        share = share - jnp.sum(pair_weight * magnitude)
        slope = slope.at[row].add(-pair_weight * pulled)
    return share, slope


CHUNKS = 8


def reduce_kernel(
    places, product, decoder, out, decoder_out, chunk_slot, member_send, member_recv,
    decoder_send, decoder_recv, first_recv, *rest
):
    groups, bits = places
    sends, recvs = rest[-2:]
    rest = list(rest[:-2])
    me, here = lax.axis_index("token"), lax.axis_index("member")
    low_bits = min(bits, CHUNKS.bit_length() - 1)
    chunks = 1 << low_bits
    width = product.shape[-1]
    half = width // 2
    piece = width // groups
    started = []

    def flip(bit):
        return me + (1 << bit) * (1 - 2 * (lax.div(me, 1 << bit) % 2))

    def bit_of(bit):
        return lax.div(me, 1 << bit) % 2

    def across(low):
        target = me
        for bit in range(low_bits):
            if low >> bit & 1:
                target = target + (1 << bit) * (1 - 2 * bit_of(bit))
        return target

    def send(source, target, device):
        index = len(started)
        copy = pltpu.make_async_remote_copy(
            src_ref=source, dst_ref=target, send_sem=sends.at[index], recv_sem=recvs.at[index],
            device_id=device, device_id_type=pl.DeviceIdType.MESH,
        )
        copy.start()
        started.append(copy)
        return copy

    barrier = pltpu.get_barrier_semaphore()
    token_partners = [across(low) for low in range(1, chunks)]
    token_partners += [flip(bit) for bit in range(low_bits, bits)]
    for partner in token_partners:
        pl.semaphore_signal(
            barrier, inc=1, device_id={"token": partner}, device_id_type=pl.DeviceIdType.MESH
        )
    for ahead in range(1, groups):
        pl.semaphore_signal(
            barrier, inc=1, device_id={"member": lax.rem(here + ahead, groups)},
            device_id_type=pl.DeviceIdType.MESH,
        )
    pl.semaphore_wait(barrier, len(token_partners) + groups - 1)

    copy0 = send(product.at[:, 1 - bit_of(0)], first_recv, {"token": flip(0)})
    lanes = []
    for part, order in enumerate((range(1, bits), range(bits - 1, 0, -1))):
        columns = pl.ds(part * half, half)
        lanes.append(dict(columns=columns, order=list(order), low=part == 0, part=part))
    blocks = 1 << (bits - 1)
    mine0 = bit_of(0)

    dec_send = decoder.at[:, 1 - mine0]
    dec_recv = rest.pop(0)
    dec_copy = send(dec_send, dec_recv, {"token": flip(0)})

    copy0.wait_recv()
    for lane in lanes:
        columns = lane["columns"]
        lane["value"] = lambda q, columns=columns: (
            product[q, mine0, :, columns].astype(jnp.float32)
            + first_recv[q, :, columns].astype(jnp.float32)
        )
    dec_copy.wait_recv()
    decoder_value = lambda q, recv=dec_recv: decoder[q, mine0] + recv[q]

    for step in range(bits - 1):
        blocks //= 2
        for lane in lanes:
            bit = lane["order"][step]
            mine = bit_of(bit)
            place = (
                (lambda q, b: 2 * q + b) if lane["low"] else (lambda q, b, n=blocks: b * n + q)
            )
            send_buf, keep, recv = rest.pop(0), rest.pop(0), rest.pop(0)
            for q in range(blocks):
                send_buf[q] = lane["value"](place(q, 1 - mine)).astype(jnp.bfloat16)
            lane["copy"] = send(send_buf, recv, {"token": flip(bit)})
            for q in range(blocks):
                keep[q] = lane["value"](place(q, mine))
            lane["value"] = lambda q, keep=keep, recv=recv: keep[q] + recv[q].astype(jnp.float32)
        bit = step + 1
        mine = bit_of(bit)
        count = chunks >> (bit + 1) if bit < low_bits else 1
        send_buf, keep, recv = rest.pop(0), rest.pop(0), rest.pop(0)
        if bit < low_bits:
            for q in range(count):
                send_buf[q] = decoder_value(2 * q + 1 - mine)
                keep[q] = decoder_value(2 * q + mine)
        else:
            send_buf[0] = decoder_value(0)
            keep[0] = send_buf[0]
        dec_copy = send(send_buf, recv, {"token": flip(bit)})
        decoder_value = lambda q, keep=keep, recv=recv: keep[q] + recv[q]
        for lane in lanes:
            lane["copy"].wait_recv()
        dec_copy.wait_recv()

    own_total, own_decoder = rest.pop(0), rest.pop(0)
    for lane in lanes:
        total = lane["value"](0)
        for index in range(groups // 2):
            spot = lane["part"] * (groups // 2) + index
            own_total[spot] = total[:, index * piece : (index + 1) * piece]
            member_send[spot] = own_total[spot].astype(jnp.bfloat16)
    total = decoder_value(0)
    for index in range(groups):
        own_decoder[index] = total[:, index * piece : (index + 1) * piece]
    waits = []
    for ahead in range(1, groups):
        target = lax.rem(here + ahead, groups)
        waits.append(send(member_send.at[target], member_recv.at[ahead - 1], {"member": target}))
        waits.append(send(own_decoder.at[target], decoder_recv.at[ahead - 1], {"member": target}))
    for copy in waits:
        copy.wait_recv()
    summed = own_total[here]
    chunk = own_decoder[here]
    for ahead in range(groups - 1):
        summed = summed + member_recv[ahead].astype(jnp.float32)
        chunk = chunk + decoder_recv[ahead]
    gathered = rest.pop(0)
    gathered[here] = summed.astype(jnp.bfloat16)
    decoder_send[here] = chunk
    back, dec_back = [], []
    for ahead in range(1, groups):
        target = lax.rem(here + ahead, groups)
        dec_back.append(send(decoder_send.at[here], decoder_send.at[here], {"member": target}))
        back.append(send(gathered.at[here], gathered.at[here], {"member": target}))
    for copy in dec_back:
        copy.wait_recv()
    mine = lax.rem(me, chunks)
    for index in range(groups):
        chunk_slot[mine, :, index * piece : (index + 1) * piece] = decoder_send[index]
    last = [
        send(chunk_slot.at[mine], chunk_slot.at[mine], {"token": across(low)})
        for low in range(1, chunks)
    ]
    for copy in back:
        copy.wait_recv()
    for index in range(groups):
        out[:, index * piece : (index + 1) * piece] = gathered[index].astype(jnp.float32)
    for copy in last:
        copy.wait_recv()
    decoder_out[...] = chunk_slot[...]
    for copy in started:
        copy.wait_send()


def reduce_gradients(product, decoder):
    count, groups = lax.axis_size("token"), lax.axis_size("member")
    bits = count.bit_length() - 1
    low_bits = min(bits, CHUNKS.bit_length() - 1)
    chunks = 1 << low_bits
    width = product.shape[1]
    rows = product.shape[0] // count
    piece, half = width // groups, width // 2
    deep = -(-decoder.shape[0] // (8 * chunks)) * 8
    padded = jnp.pad(decoder, ((0, deep * chunks - decoder.shape[0]), (0, 0)))
    f32, bf16 = jnp.float32, jnp.bfloat16
    scratch = [
        pltpu.VMEM((chunks, deep, width), f32),
        pltpu.VMEM((groups, rows, piece), bf16),
        pltpu.VMEM((groups - 1, rows, piece), bf16),
        pltpu.VMEM((groups, deep, piece), f32),
        pltpu.VMEM((groups - 1, deep, piece), f32),
        pltpu.VMEM((count // 2, rows, width), bf16),
        pltpu.VMEM((chunks // 2, deep, width), f32),
    ]
    blocks = count // 2
    copies = 2
    for step in range(bits - 1):
        blocks //= 2
        for _ in range(2):
            scratch += [
                pltpu.VMEM((blocks, rows, half), bf16),
                pltpu.VMEM((blocks, rows, half), f32),
                pltpu.VMEM((blocks, rows, half), bf16),
            ]
        left = max(chunks >> (step + 2), 1)
        scratch += [pltpu.VMEM((left, deep, width), f32)] * 3
        copies += 3
    scratch += [
        pltpu.VMEM((groups, rows, piece), f32),
        pltpu.VMEM((groups, deep, piece), f32),
        pltpu.VMEM((groups, rows, piece), bf16),
    ]
    copies += 4 * (groups - 1) + chunks - 1
    scratch += [pltpu.SemaphoreType.DMA((copies,)), pltpu.SemaphoreType.DMA((copies,))]
    out, whole = pl.pallas_call(
        functools.partial(reduce_kernel, (groups, bits)),
        out_shape=(
            jax.ShapeDtypeStruct((rows, width), f32),
            jax.ShapeDtypeStruct((chunks, deep, width), f32),
        ),
        in_specs=[pl.BlockSpec(memory_space=pltpu.VMEM)] * 2,
        out_specs=[pl.BlockSpec(memory_space=pltpu.VMEM)] * 2,
        scratch_shapes=scratch,
        compiler_params=pltpu.CompilerParams(
            collective_id=0, has_side_effects=True, vmem_limit_bytes=40 * 2**20
        ),
    )(
        product.reshape(count // 2, 2, rows, width),
        padded.reshape(chunks // 2, 2, deep, width),
    )
    return out, whole.reshape(chunks * deep, width)


def shards(
    members_in,
    member_noise,
    norm_gain,
    weight_query,
    weight_key,
    weight_value,
    weight_out,
    decoder_projection_weight,
    decoder_bias,
    observations,
    surface_extent_factor,
    quantity_scoring_factor,
    point_map,
):
    member_rows, tokens, width = members_in.shape
    state = members_in.astype(jnp.float32)

    def front(state_in):
        return project(state_in, member_noise, norm_gain, weight_query, weight_key, weight_value)

    (query, key, value), front_pull = jax.vjp(front, state)
    stacked = jnp.stack([key, value])
    extended = extended_2(stacked, (("token", 2),), HALF)
    leading_realization = lax.axis_index("token") * tokens
    total = tokens * lax.axis_size("token")

    def middle(query_in, extended_in):
        return attend(query_in, extended_in[0], extended_in[1], leading_realization, total)

    attended, middle_pull = jax.vjp(middle, query, extended)
    flat_att = attended.reshape(member_rows * tokens, width)
    update = jnp.dot(flat_att, weight_out, preferred_element_type=jnp.float32).reshape(
        member_rows, tokens, width
    )
    residual_stream_state = (state + member_noise.astype(jnp.float32) + update).astype(jnp.bfloat16)

    own = jnp.einsum(
        "vc,mtc->mvt",
        decoder_projection_weight,
        residual_stream_state,
        preferred_element_type=jnp.float32,
    )
    own = own + decoder_bias[None, :, None]
    share, slope = score_and_slope(
        own, observations, surface_extent_factor, quantity_scoring_factor, point_map
    )
    slope = slope.astype(jnp.bfloat16)
    decoder_piece = jnp.einsum(
        "mvt,mtc->vc", slope, residual_stream_state, preferred_element_type=jnp.float32
    )
    carried_slope = jnp.einsum(
        "mvt,vc->mtc", slope, decoder_projection_weight, preferred_element_type=jnp.float32
    ).astype(jnp.bfloat16)
    flat_grad = carried_slope.reshape(member_rows * tokens, width)
    grad_attended = (
        jnp.dot(flat_grad, weight_out.T, preferred_element_type=jnp.float32)
        .astype(jnp.bfloat16)
        .reshape(member_rows, tokens, width)
    )
    grad_query, grad_extended = middle_pull(grad_attended)
    lower_rim = grad_extended[:, :, :HALF]
    upper_rim = grad_extended[:, :, tokens + HALF :]
    inner = grad_extended[:, :, HALF : tokens + HALF].astype(jnp.float32)
    from_next = from_behind(lower_rim, "token", -1)
    from_prev = from_behind(upper_rim, "token", 1)
    inner = inner.at[:, :, tokens - HALF :].add(from_next.astype(jnp.float32))
    inner = inner.at[:, :, :HALF].add(from_prev.astype(jnp.float32))
    (grad_front,) = front_pull(
        (grad_query, inner[0].astype(jnp.bfloat16), inner[1].astype(jnp.bfloat16))
    )
    grad_members = (grad_front + carried_slope.astype(jnp.float32)).astype(jnp.bfloat16)
    contract = (((0,), (0,)), ((), ()))
    product = lax.dot_general(flat_att, flat_grad, contract, preferred_element_type=jnp.float32)
    variables = decoder_piece.shape[0]
    decoder_piece = jnp.concatenate([decoder_piece, jnp.full((1, width), share)])
    grad_out, decoder_sum = reduce_gradients(product.astype(jnp.bfloat16), decoder_piece)
    grad_decoder = decoder_sum[:variables]
    mean_scoring = decoder_sum[variables, 0] / (
        observations.shape[0] * observations.shape[1] * lax.axis_size("token")
    )
    return (mean_scoring, grad_members, grad_out, grad_decoder)


def solution(mesh):
    return jax.shard_map(
        shards,
        mesh=mesh,
        in_specs=(
            P("member", "token", None),
            P("member", "token", None),
            P(),
            P(),
            P(),
            P(),
            P(),
            P(),
            P(),
            P(None, "token"),
            P("token"),
            P(),
            P("token"),
        ),
        out_specs=(P(), P("member", "token", None), P("token", None), P()),
        check_vma=False,
    )
```

```python
import functools

import jax
import jax.numpy as jnp
from jax import lax
from jax.experimental import pallas as pl
from jax.experimental.pallas import tpu as pltpu
from jax.sharding import PartitionSpec as P

HEADS = 16
HALF = 128


EPSILON = 1e-06
SMOOTH = 0.01


def from_behind(block, axis, distance):
    devices = range(lax.axis_size(axis))
    route = [(i - distance, i) for i in devices if i - distance in devices]
    return lax.ppermute(block, axis, route)


def normalize_heads(flat):
    rows, width = flat.shape
    split = flat.reshape(rows, HEADS, width // HEADS)
    split = split * lax.rsqrt(jnp.mean(split * split, axis=-1, keepdims=True) + EPSILON)
    return split.reshape(rows, width)


def project(state_in, member_noise, norm_gain, weight_query, weight_key, weight_value):
    member_rows, tokens, width = state_in.shape
    mixed = state_in + member_noise.astype(jnp.float32)
    normed = (
        mixed * lax.rsqrt(jnp.mean(mixed * mixed, axis=-1, keepdims=True) + EPSILON) * norm_gain
    ).astype(jnp.bfloat16)
    flat = normed.reshape(member_rows * tokens, width)
    query = normalize_heads(jnp.dot(flat, weight_query, preferred_element_type=jnp.float32)).astype(
        jnp.bfloat16
    )
    key = normalize_heads(jnp.dot(flat, weight_key, preferred_element_type=jnp.float32)).astype(
        jnp.bfloat16
    )
    value = jnp.dot(flat, weight_value, preferred_element_type=jnp.float32).astype(jnp.bfloat16)
    full_shape = (member_rows, tokens, width)
    return (query.reshape(full_shape), key.reshape(full_shape), value.reshape(full_shape))


LANES = 256


def lane_pairs(depth):
    lane = lax.broadcasted_iota(jnp.int32, (1, 128), 1)
    return [(lane >= first) & (lane < first + depth) for first in range(0, 128, depth)]


def allowed_keys(tokens):
    index, count = lax.axis_index("token"), lax.axis_size("token")
    row = lax.broadcasted_iota(jnp.int32, (tokens, 3 * tokens), 0)
    column = lax.broadcasted_iota(jnp.int32, (tokens, 3 * tokens), 1)
    least = jnp.where(index == 0, tokens, 0)
    most = jnp.where(index == count - 1, 2 * tokens, 3 * tokens)
    window = (column >= row) & (column < row + 2 * HALF)
    return window & (column >= least) & (column < most)


def product_of(left, right, left_dim, right_dim):
    return lax.dot_general(
        left, right, (((left_dim,), (right_dim,)), ((), ())), preferred_element_type=jnp.float32
    )


def raised_of(query, keys, allowed, scale):
    raised = jnp.where(allowed, jnp.exp(product_of(query, keys, 1, 1) * scale), 0.0)
    return raised / jnp.sum(raised, axis=-1, keepdims=True)


def attend_kernel(depth, query, below, own, above, out):
    tokens = query.shape[1]
    allowed = allowed_keys(tokens)
    scale = depth**-0.5
    for first in range(0, LANES, 128):
        lanes = slice(first, first + 128)
        keys, values = (
            jnp.concatenate([block[kind, 0, :, lanes] for block in (below, own, above)], axis=0)
            for kind in (0, 1)
        )
        mixed = jnp.zeros((tokens, 128), jnp.float32)
        for chosen in lane_pairs(depth):
            picked = jnp.where(chosen, query[0, :, lanes], 0)
            probs = raised_of(picked, keys, allowed, scale).astype(jnp.bfloat16)
            mixed = jnp.where(chosen, product_of(probs, values, 1, 0), mixed)
        out[0, :, lanes] = mixed.astype(jnp.bfloat16)


def attend_back_kernel(
    depth, query, below, own, above, slope, query_out, below_out, own_out, above_out
):
    tokens = query.shape[1]
    allowed = allowed_keys(tokens)
    scale = depth**-0.5
    for first in range(0, LANES, 128):
        lanes = slice(first, first + 128)
        keys, values = (
            jnp.concatenate([block[kind, 0, :, lanes] for block in (below, own, above)], axis=0)
            for kind in (0, 1)
        )
        query_slope = jnp.zeros((tokens, 128), jnp.float32)
        key_slope = jnp.zeros((3 * tokens, 128), jnp.float32)
        value_slope = jnp.zeros((3 * tokens, 128), jnp.float32)
        for chosen in lane_pairs(depth):
            picked = jnp.where(chosen, query[0, :, lanes], 0)
            pulled = jnp.where(chosen, slope[0, :, lanes], 0)
            probs = raised_of(picked, keys, allowed, scale)
            weight = product_of(pulled, values, 1, 1)
            mean = jnp.sum(weight * probs, axis=-1, keepdims=True)
            score_slope = (probs * (weight - mean) * scale).astype(jnp.bfloat16)
            query_slope = jnp.where(chosen, product_of(score_slope, keys, 1, 0), query_slope)
            key_slope = key_slope + product_of(score_slope, picked, 0, 0)
            value_slope = value_slope + product_of(probs.astype(jnp.bfloat16), pulled, 0, 0)
        query_out[0, :, lanes] = query_slope.astype(jnp.bfloat16)
        for kind, total in ((0, key_slope), (1, value_slope)):
            below_out[kind, 0, :, lanes] = total[:tokens].astype(jnp.bfloat16)
            own_out[kind, 0, :, lanes] = total[tokens : 2 * tokens]
            above_out[kind, 0, :, lanes] = total[2 * tokens :].astype(jnp.bfloat16)


def attention(query, below, own, above, slope=None):
    members, tokens, width = query.shape
    assert tokens == HALF
    depth = width // HEADS
    flat = pl.BlockSpec((1, tokens, LANES), lambda m, h: (m, 0, h))
    pair = pl.BlockSpec((2, 1, tokens, LANES), lambda m, h: (0, m, 0, h))
    size = members * tokens * 3 * tokens * width
    half = jax.ShapeDtypeStruct(query.shape, jnp.bfloat16)
    pairs = [
        jax.ShapeDtypeStruct(own.shape, kind) for kind in (jnp.bfloat16, jnp.float32, jnp.bfloat16)
    ]
    if slope is None:
        return pl.pallas_call(
            functools.partial(attend_kernel, depth),
            grid=(members, width // LANES),
            out_shape=half,
            in_specs=[flat, pair, pair, pair],
            out_specs=flat,
            compiler_params=pltpu.CompilerParams(vmem_limit_bytes=24 * 2**20),
            cost_estimate=pl.CostEstimate(
                flops=4 * size, bytes_accessed=16 * query.size, transcendentals=size // depth
            ),
        )(query, below, own, above)
    return pl.pallas_call(
        functools.partial(attend_back_kernel, depth),
        grid=(members, width // LANES),
        out_shape=[half, *pairs],
        in_specs=[flat, pair, pair, pair, flat],
        out_specs=[flat, pair, pair, pair],
        compiler_params=pltpu.CompilerParams(vmem_limit_bytes=24 * 2**20),
        cost_estimate=pl.CostEstimate(
            flops=10 * size, bytes_accessed=36 * query.size, transcendentals=size // depth
        ),
    )(query, below, own, above, slope)


def split_product(left, right, equation):
    high = left.astype(jnp.bfloat16)
    low = (left - high.astype(jnp.float32)).astype(jnp.bfloat16)
    first = jnp.einsum(equation, high, right, preferred_element_type=jnp.float32)
    return first + jnp.einsum(equation, low, right, preferred_element_type=jnp.float32)


def score_and_slope(own, observed, surface_extent, quantity, point_map):
    member_rows, _, tokens = own.shape
    onehot = point_map[:, None] == lax.iota(jnp.int32, tokens)[None, :]
    token_area = jnp.sum(jnp.where(onehot, surface_extent[:, None], 0.0), axis=0)
    onehot = onehot.astype(jnp.bfloat16)
    everyone = lax.all_gather(own, "member", axis=0, tiled=True)
    count = everyone.shape[0]
    diff = split_product(own, onehot, "mvt,pt->mvp") - observed[None]
    inverse = lax.rsqrt(diff * diff + SMOOTH)
    weight = quantity[:, None] * surface_extent[None, :] / count
    weighted = weight[None] * inverse
    share = jnp.sum(weighted * (diff * diff + SMOOTH))
    slope = split_product(weighted * diff, onehot, "mvp,pt->mvt")
    first = lax.axis_index("member") * member_rows
    pair_weight = quantity[:, None] * token_area[None, :] / (count * (count - 1))
    for row in range(member_rows):
        magnitude = jnp.zeros_like(own[0])
        pulled = jnp.zeros_like(own[0])
        for other in range(count):
            gap = own[row] - everyone[other]
            square = gap * gap + SMOOTH
            upside = lax.rsqrt(square)
            keep = jnp.where(first + row == other, 0.0, 0.5)
            magnitude = magnitude + keep * square * upside
            pulled = pulled + gap * upside
        share = share - jnp.sum(pair_weight * magnitude)
        slope = slope.at[row].add(-pair_weight * pulled)
    return share, slope


CHUNKS = 8


def reduce_kernel(
    places, product, decoder, out, decoder_out, chunk_slot, member_send, member_recv,
    decoder_send, decoder_recv, first_recv, *rest
):
    groups, bits = places
    sends, recvs = rest[-2:]
    rest = list(rest[:-2])
    me, here = lax.axis_index("token"), lax.axis_index("member")
    low_bits = min(bits, CHUNKS.bit_length() - 1)
    chunks = 1 << low_bits
    width = product.shape[-1]
    half = width // 2
    piece = width // groups
    started = []

    def flip(bit):
        return me + (1 << bit) * (1 - 2 * (lax.div(me, 1 << bit) % 2))

    def bit_of(bit):
        return lax.div(me, 1 << bit) % 2

    def across(low):
        target = me
        for bit in range(low_bits):
            if low >> bit & 1:
                target = target + (1 << bit) * (1 - 2 * bit_of(bit))
        return target

    def send(source, target, device):
        index = len(started)
        copy = pltpu.make_async_remote_copy(
            src_ref=source, dst_ref=target, send_sem=sends.at[index], recv_sem=recvs.at[index],
            device_id=device, device_id_type=pl.DeviceIdType.MESH,
        )
        copy.start()
        started.append(copy)
        return copy

    barrier = pltpu.get_barrier_semaphore()
    token_partners = [across(low) for low in range(1, chunks)]
    token_partners += [flip(bit) for bit in range(low_bits, bits)]
    for partner in token_partners:
        pl.semaphore_signal(
            barrier, inc=1, device_id={"token": partner}, device_id_type=pl.DeviceIdType.MESH
        )
    for ahead in range(1, groups):
        pl.semaphore_signal(
            barrier, inc=1, device_id={"member": lax.rem(here + ahead, groups)},
            device_id_type=pl.DeviceIdType.MESH,
        )
    pl.semaphore_wait(barrier, len(token_partners) + groups - 1)

    copy0 = send(product.at[:, 1 - bit_of(0)], first_recv, {"token": flip(0)})
    lanes = []
    for part, order in enumerate((range(1, bits), range(bits - 1, 0, -1))):
        columns = pl.ds(part * half, half)
        lanes.append(dict(columns=columns, order=list(order), low=part == 0, part=part))
    blocks = 1 << (bits - 1)
    mine0 = bit_of(0)

    dec_send = decoder.at[:, 1 - mine0]
    dec_recv = rest.pop(0)
    dec_copy = send(dec_send, dec_recv, {"token": flip(0)})

    copy0.wait_recv()
    for lane in lanes:
        columns = lane["columns"]
        lane["value"] = lambda q, columns=columns: (
            product[q, mine0, :, columns].astype(jnp.float32)
            + first_recv[q, :, columns].astype(jnp.float32)
        )
    dec_copy.wait_recv()
    decoder_value = lambda q, recv=dec_recv: decoder[q, mine0] + recv[q]

    for step in range(bits - 1):
        blocks //= 2
        for lane in lanes:
            bit = lane["order"][step]
            mine = bit_of(bit)
            place = (
                (lambda q, b: 2 * q + b) if lane["low"] else (lambda q, b, n=blocks: b * n + q)
            )
            send_buf, keep, recv = rest.pop(0), rest.pop(0), rest.pop(0)
            for q in range(blocks):
                send_buf[q] = lane["value"](place(q, 1 - mine)).astype(jnp.bfloat16)
            lane["copy"] = send(send_buf, recv, {"token": flip(bit)})
            for q in range(blocks):
                keep[q] = lane["value"](place(q, mine))
            lane["value"] = lambda q, keep=keep, recv=recv: keep[q] + recv[q].astype(jnp.float32)
        bit = step + 1
        mine = bit_of(bit)
        count = chunks >> (bit + 1) if bit < low_bits else 1
        send_buf, keep, recv = rest.pop(0), rest.pop(0), rest.pop(0)
        if bit < low_bits:
            for q in range(count):
                send_buf[q] = decoder_value(2 * q + 1 - mine)
                keep[q] = decoder_value(2 * q + mine)
        else:
            send_buf[0] = decoder_value(0)
            keep[0] = send_buf[0]
        dec_copy = send(send_buf, recv, {"token": flip(bit)})
        decoder_value = lambda q, keep=keep, recv=recv: keep[q] + recv[q]
        for lane in lanes:
            lane["copy"].wait_recv()
        dec_copy.wait_recv()

    own_total, own_decoder = rest.pop(0), rest.pop(0)
    for lane in lanes:
        total = lane["value"](0)
        for index in range(groups // 2):
            spot = lane["part"] * (groups // 2) + index
            own_total[spot] = total[:, index * piece : (index + 1) * piece]
            member_send[spot] = own_total[spot].astype(jnp.bfloat16)
    total = decoder_value(0)
    for index in range(groups):
        own_decoder[index] = total[:, index * piece : (index + 1) * piece]
    waits = []
    for ahead in range(1, groups):
        target = lax.rem(here + ahead, groups)
        waits.append(send(member_send.at[target], member_recv.at[ahead - 1], {"member": target}))
        waits.append(send(own_decoder.at[target], decoder_recv.at[ahead - 1], {"member": target}))
    for copy in waits:
        copy.wait_recv()
    summed = own_total[here]
    chunk = own_decoder[here]
    for ahead in range(groups - 1):
        summed = summed + member_recv[ahead].astype(jnp.float32)
        chunk = chunk + decoder_recv[ahead]
    gathered = rest.pop(0)
    gathered[here] = summed.astype(jnp.bfloat16)
    decoder_send[here] = chunk
    back, dec_back = [], []
    for ahead in range(1, groups):
        target = lax.rem(here + ahead, groups)
        dec_back.append(send(decoder_send.at[here], decoder_send.at[here], {"member": target}))
        back.append(send(gathered.at[here], gathered.at[here], {"member": target}))
    for copy in dec_back:
        copy.wait_recv()
    mine = lax.rem(me, chunks)
    for index in range(groups):
        chunk_slot[mine, :, index * piece : (index + 1) * piece] = decoder_send[index]
    last = [
        send(chunk_slot.at[mine], chunk_slot.at[mine], {"token": across(low)})
        for low in range(1, chunks)
    ]
    for copy in back:
        copy.wait_recv()
    for index in range(groups):
        out[:, index * piece : (index + 1) * piece] = gathered[index].astype(jnp.float32)
    for copy in last:
        copy.wait_recv()
    decoder_out[...] = chunk_slot[...]
    for copy in started:
        copy.wait_send()


def reduce_gradients(product, decoder):
    count, groups = lax.axis_size("token"), lax.axis_size("member")
    bits = count.bit_length() - 1
    low_bits = min(bits, CHUNKS.bit_length() - 1)
    chunks = 1 << low_bits
    width = product.shape[1]
    rows = product.shape[0] // count
    piece, half = width // groups, width // 2
    deep = -(-decoder.shape[0] // (8 * chunks)) * 8
    padded = jnp.pad(decoder, ((0, deep * chunks - decoder.shape[0]), (0, 0)))
    f32, bf16 = jnp.float32, jnp.bfloat16
    scratch = [
        pltpu.VMEM((chunks, deep, width), f32),
        pltpu.VMEM((groups, rows, piece), bf16),
        pltpu.VMEM((groups - 1, rows, piece), bf16),
        pltpu.VMEM((groups, deep, piece), f32),
        pltpu.VMEM((groups - 1, deep, piece), f32),
        pltpu.VMEM((count // 2, rows, width), bf16),
        pltpu.VMEM((chunks // 2, deep, width), f32),
    ]
    blocks = count // 2
    copies = 2
    for step in range(bits - 1):
        blocks //= 2
        for _ in range(2):
            scratch += [
                pltpu.VMEM((blocks, rows, half), bf16),
                pltpu.VMEM((blocks, rows, half), f32),
                pltpu.VMEM((blocks, rows, half), bf16),
            ]
        left = max(chunks >> (step + 2), 1)
        scratch += [pltpu.VMEM((left, deep, width), f32)] * 3
        copies += 3
    scratch += [
        pltpu.VMEM((groups, rows, piece), f32),
        pltpu.VMEM((groups, deep, piece), f32),
        pltpu.VMEM((groups, rows, piece), bf16),
    ]
    copies += 4 * (groups - 1) + chunks - 1
    scratch += [pltpu.SemaphoreType.DMA((copies,)), pltpu.SemaphoreType.DMA((copies,))]
    out, whole = pl.pallas_call(
        functools.partial(reduce_kernel, (groups, bits)),
        out_shape=(
            jax.ShapeDtypeStruct((rows, width), f32),
            jax.ShapeDtypeStruct((chunks, deep, width), f32),
        ),
        in_specs=[pl.BlockSpec(memory_space=pltpu.VMEM)] * 2,
        out_specs=[pl.BlockSpec(memory_space=pltpu.VMEM)] * 2,
        scratch_shapes=scratch,
        compiler_params=pltpu.CompilerParams(
            collective_id=0, has_side_effects=True, vmem_limit_bytes=40 * 2**20
        ),
    )(
        product.reshape(count // 2, 2, rows, width),
        padded.reshape(chunks // 2, 2, deep, width),
    )
    return out, whole.reshape(chunks * deep, width)


def shards(
    members_in,
    member_noise,
    norm_gain,
    weight_query,
    weight_key,
    weight_value,
    weight_out,
    decoder_projection_weight,
    decoder_bias,
    observations,
    surface_extent_factor,
    quantity_scoring_factor,
    point_map,
):
    member_rows, tokens, width = members_in.shape
    state = members_in.astype(jnp.float32)

    def front(state_in):
        return project(state_in, member_noise, norm_gain, weight_query, weight_key, weight_value)

    (query, key, value), front_pull = jax.vjp(front, state)
    stacked = jnp.stack([key, value])
    below = from_behind(stacked, "token", 1)
    above = from_behind(stacked, "token", -1)
    attended = attention(query, below, stacked, above)
    flat_att = attended.reshape(member_rows * tokens, width)
    update = jnp.dot(flat_att, weight_out, preferred_element_type=jnp.float32).reshape(
        member_rows, tokens, width
    )
    residual_stream_state = (state + member_noise.astype(jnp.float32) + update).astype(jnp.bfloat16)

    own = jnp.einsum(
        "vc,mtc->mvt",
        decoder_projection_weight,
        residual_stream_state,
        preferred_element_type=jnp.float32,
    )
    own = own + decoder_bias[None, :, None]
    share, slope = score_and_slope(
        own, observations, surface_extent_factor, quantity_scoring_factor, point_map
    )
    slope = slope.astype(jnp.bfloat16)
    decoder_piece = jnp.einsum(
        "mvt,mtc->vc", slope, residual_stream_state, preferred_element_type=jnp.float32
    )
    carried_slope = jnp.einsum(
        "mvt,vc->mtc", slope, decoder_projection_weight, preferred_element_type=jnp.float32
    ).astype(jnp.bfloat16)
    flat_grad = carried_slope.reshape(member_rows * tokens, width)
    grad_attended = (
        jnp.dot(flat_grad, weight_out.T, preferred_element_type=jnp.float32)
        .astype(jnp.bfloat16)
        .reshape(member_rows, tokens, width)
    )
    grad_query, lower_rim, inner, upper_rim = attention(
        query, below, stacked, above, grad_attended
    )
    from_next = from_behind(lower_rim, "token", -1)
    from_prev = from_behind(upper_rim, "token", 1)
    inner = inner + from_next.astype(jnp.float32) + from_prev.astype(jnp.float32)
    (grad_front,) = front_pull(
        (grad_query, inner[0].astype(jnp.bfloat16), inner[1].astype(jnp.bfloat16))
    )
    grad_members = (grad_front + carried_slope.astype(jnp.float32)).astype(jnp.bfloat16)
    contract = (((0,), (0,)), ((), ()))
    product = lax.dot_general(flat_att, flat_grad, contract, preferred_element_type=jnp.float32)
    variables = decoder_piece.shape[0]
    decoder_piece = jnp.concatenate([decoder_piece, jnp.full((1, width), share)])
    grad_out, decoder_sum = reduce_gradients(product.astype(jnp.bfloat16), decoder_piece)
    grad_decoder = decoder_sum[:variables]
    mean_scoring = decoder_sum[variables, 0] / (
        observations.shape[0] * observations.shape[1] * lax.axis_size("token")
    )
    return (mean_scoring, grad_members, grad_out, grad_decoder)


def solution(mesh):
    return jax.shard_map(
        shards,
        mesh=mesh,
        in_specs=(
            P("member", "token", None),
            P("member", "token", None),
            P(),
            P(),
            P(),
            P(),
            P(),
            P(),
            P(),
            P(None, "token"),
            P("token"),
            P(),
            P("token"),
        ),
        out_specs=(P(), P("member", "token", None), P("token", None), P()),
        check_vma=False,
    )
```

```python
import functools

import jax
import jax.numpy as jnp
from jax import lax
from jax.experimental import pallas as pl
from jax.experimental.pallas import tpu as pltpu
from jax.sharding import PartitionSpec as P

HEADS = 16
HALF = 128


EPSILON = 1e-06
SMOOTH = 0.01


def from_behind(block, axis, distance):
    devices = range(lax.axis_size(axis))
    route = [(i - distance, i) for i in devices if i - distance in devices]
    return lax.ppermute(block, axis, route)


def head_places(width):
    feature = lax.broadcasted_iota(jnp.int32, (width, HEADS), 0) // (width // HEADS)
    return (feature == lax.broadcasted_iota(jnp.int32, (width, HEADS), 1)).astype(jnp.bfloat16)


def head_mean(flat):
    width = flat.shape[1]
    return split_product(flat, head_places(width), "rc,ch->rh") * (HEADS / width)


def over_heads(each, width):
    return split_product(each, head_places(width), "rh,ch->rc")


@jax.custom_vjp
def normalize_heads(flat):
    return normalize_heads_forward(flat)[0]


def normalize_heads_forward(flat):
    inverse = lax.rsqrt(head_mean(flat * flat) + EPSILON)
    return flat * over_heads(inverse, flat.shape[1]), (flat, inverse)


def normalize_heads_back(saved, slope):
    flat, inverse = saved
    width = flat.shape[1]
    pulled = head_mean(slope * flat) * inverse * inverse * inverse
    return (slope * over_heads(inverse, width) - flat * over_heads(pulled, width),)


normalize_heads.defvjp(normalize_heads_forward, normalize_heads_back)


def project(state_in, member_noise, norm_gain, weight_query, weight_key, weight_value):
    member_rows, tokens, width = state_in.shape
    mixed = state_in + member_noise.astype(jnp.float32)
    normed = (
        mixed * lax.rsqrt(jnp.mean(mixed * mixed, axis=-1, keepdims=True) + EPSILON) * norm_gain
    ).astype(jnp.bfloat16)
    flat = normed.reshape(member_rows * tokens, width)
    query = normalize_heads(jnp.dot(flat, weight_query, preferred_element_type=jnp.float32)).astype(
        jnp.bfloat16
    )
    key = normalize_heads(jnp.dot(flat, weight_key, preferred_element_type=jnp.float32)).astype(
        jnp.bfloat16
    )
    value = jnp.dot(flat, weight_value, preferred_element_type=jnp.float32).astype(jnp.bfloat16)
    full_shape = (member_rows, tokens, width)
    return (query.reshape(full_shape), key.reshape(full_shape), value.reshape(full_shape))


LANES = 256


def lane_pairs(depth):
    lane = lax.broadcasted_iota(jnp.int32, (1, 128), 1)
    return [(lane >= first) & (lane < first + depth) for first in range(0, 128, depth)]


def allowed_keys(tokens):
    index, count = lax.axis_index("token"), lax.axis_size("token")
    row = lax.broadcasted_iota(jnp.int32, (tokens, 3 * tokens), 0)
    column = lax.broadcasted_iota(jnp.int32, (tokens, 3 * tokens), 1)
    least = jnp.where(index == 0, tokens, 0)
    most = jnp.where(index == count - 1, 2 * tokens, 3 * tokens)
    window = (column >= row) & (column < row + 2 * HALF)
    return window & (column >= least) & (column < most)


def product_of(left, right, left_dim, right_dim):
    return lax.dot_general(
        left, right, (((left_dim,), (right_dim,)), ((), ())), preferred_element_type=jnp.float32
    )


def raised_of(query, keys, allowed, scale):
    raised = jnp.where(allowed, jnp.exp(product_of(query, keys, 1, 1) * scale), 0.0)
    return raised / jnp.sum(raised, axis=-1, keepdims=True)


def attend_kernel(depth, query, below, own, above, out):
    tokens = query.shape[1]
    allowed = allowed_keys(tokens)
    scale = depth**-0.5
    for first in range(0, LANES, 128):
        lanes = slice(first, first + 128)
        keys, values = (
            jnp.concatenate([block[kind, 0, :, lanes] for block in (below, own, above)], axis=0)
            for kind in (0, 1)
        )
        mixed = jnp.zeros((tokens, 128), jnp.float32)
        for chosen in lane_pairs(depth):
            picked = jnp.where(chosen, query[0, :, lanes], 0)
            probs = raised_of(picked, keys, allowed, scale).astype(jnp.bfloat16)
            mixed = jnp.where(chosen, product_of(probs, values, 1, 0), mixed)
        out[0, :, lanes] = mixed.astype(jnp.bfloat16)


def attend_back_kernel(
    depth, query, below, own, above, slope, query_out, below_out, own_out, above_out
):
    tokens = query.shape[1]
    allowed = allowed_keys(tokens)
    scale = depth**-0.5
    for first in range(0, LANES, 128):
        lanes = slice(first, first + 128)
        keys, values = (
            jnp.concatenate([block[kind, 0, :, lanes] for block in (below, own, above)], axis=0)
            for kind in (0, 1)
        )
        query_slope = jnp.zeros((tokens, 128), jnp.float32)
        key_slope = jnp.zeros((3 * tokens, 128), jnp.float32)
        value_slope = jnp.zeros((3 * tokens, 128), jnp.float32)
        for chosen in lane_pairs(depth):
            picked = jnp.where(chosen, query[0, :, lanes], 0)
            pulled = jnp.where(chosen, slope[0, :, lanes], 0)
            probs = raised_of(picked, keys, allowed, scale)
            weight = product_of(pulled, values, 1, 1)
            mean = jnp.sum(weight * probs, axis=-1, keepdims=True)
            score_slope = (probs * (weight - mean) * scale).astype(jnp.bfloat16)
            query_slope = jnp.where(chosen, product_of(score_slope, keys, 1, 0), query_slope)
            key_slope = key_slope + product_of(score_slope, picked, 0, 0)
            value_slope = value_slope + product_of(probs.astype(jnp.bfloat16), pulled, 0, 0)
        query_out[0, :, lanes] = query_slope.astype(jnp.bfloat16)
        for kind, total in ((0, key_slope), (1, value_slope)):
            below_out[kind, 0, :, lanes] = total[:tokens].astype(jnp.bfloat16)
            own_out[kind, 0, :, lanes] = total[tokens : 2 * tokens]
            above_out[kind, 0, :, lanes] = total[2 * tokens :].astype(jnp.bfloat16)


def attention(query, below, own, above, slope=None):
    members, tokens, width = query.shape
    assert tokens == HALF
    depth = width // HEADS
    flat = pl.BlockSpec((1, tokens, LANES), lambda m, h: (m, 0, h))
    pair = pl.BlockSpec((2, 1, tokens, LANES), lambda m, h: (0, m, 0, h))
    size = members * tokens * 3 * tokens * width
    half = jax.ShapeDtypeStruct(query.shape, jnp.bfloat16)
    pairs = [
        jax.ShapeDtypeStruct(own.shape, kind) for kind in (jnp.bfloat16, jnp.float32, jnp.bfloat16)
    ]
    if slope is None:
        return pl.pallas_call(
            functools.partial(attend_kernel, depth),
            grid=(members, width // LANES),
            out_shape=half,
            in_specs=[flat, pair, pair, pair],
            out_specs=flat,
            compiler_params=pltpu.CompilerParams(vmem_limit_bytes=24 * 2**20),
            cost_estimate=pl.CostEstimate(
                flops=4 * size, bytes_accessed=16 * query.size, transcendentals=size // depth
            ),
        )(query, below, own, above)
    return pl.pallas_call(
        functools.partial(attend_back_kernel, depth),
        grid=(members, width // LANES),
        out_shape=[half, *pairs],
        in_specs=[flat, pair, pair, pair, flat],
        out_specs=[flat, pair, pair, pair],
        compiler_params=pltpu.CompilerParams(vmem_limit_bytes=24 * 2**20),
        cost_estimate=pl.CostEstimate(
            flops=10 * size, bytes_accessed=36 * query.size, transcendentals=size // depth
        ),
    )(query, below, own, above, slope)


def split_product(left, right, equation):
    high = left.astype(jnp.bfloat16)
    low = (left - high.astype(jnp.float32)).astype(jnp.bfloat16)
    first = jnp.einsum(equation, high, right, preferred_element_type=jnp.float32)
    return first + jnp.einsum(equation, low, right, preferred_element_type=jnp.float32)


def gather_kernel(groups, own, out, slots, sends, recvs):
    here = lax.axis_index("member")
    barrier = pltpu.get_barrier_semaphore()
    for ahead in range(1, groups):
        pl.semaphore_signal(
            barrier, inc=1, device_id={"member": lax.rem(here + ahead, groups)},
            device_id_type=pl.DeviceIdType.MESH,
        )
    pl.semaphore_wait(barrier, groups - 1)
    copies = []
    for ahead in range(1, groups):
        copy = pltpu.make_async_remote_copy(
            src_ref=own, dst_ref=slots.at[here],
            send_sem=sends.at[ahead - 1], recv_sem=recvs.at[ahead - 1],
            device_id={"member": lax.rem(here + ahead, groups)},
            device_id_type=pl.DeviceIdType.MESH,
        )
        copy.start()
        copies.append(copy)
    slots[here] = own[...]
    for copy in copies:
        copy.wait()
    out[...] = slots[...]


def gather_members(own):
    groups = lax.axis_size("member")
    shape = (groups, *own.shape)
    gathered = pl.pallas_call(
        functools.partial(gather_kernel, groups),
        out_shape=jax.ShapeDtypeStruct(shape, own.dtype),
        in_specs=[pl.BlockSpec(memory_space=pltpu.VMEM)],
        out_specs=pl.BlockSpec(memory_space=pltpu.VMEM),
        scratch_shapes=[
            pltpu.VMEM(shape, own.dtype),
            pltpu.SemaphoreType.DMA((groups - 1,)),
            pltpu.SemaphoreType.DMA((groups - 1,)),
        ],
        compiler_params=pltpu.CompilerParams(collective_id=1, has_side_effects=True),
    )(own)
    return gathered.reshape(groups * own.shape[0], *own.shape[1:])


def score_and_slope(own, observed, surface_extent, quantity, point_map):
    member_rows, _, tokens = own.shape
    onehot = point_map[:, None] == lax.iota(jnp.int32, tokens)[None, :]
    token_area = jnp.sum(jnp.where(onehot, surface_extent[:, None], 0.0), axis=0)
    onehot = onehot.astype(jnp.bfloat16)
    everyone = gather_members(own)
    count = everyone.shape[0]
    diff = split_product(own, onehot, "mvt,pt->mvp") - observed[None]
    inverse = lax.rsqrt(diff * diff + SMOOTH)
    weight = quantity[:, None] * surface_extent[None, :] / count
    weighted = weight[None] * inverse
    share = jnp.sum(weighted * (diff * diff + SMOOTH))
    slope = split_product(weighted * diff, onehot, "mvp,pt->mvt")
    first = lax.axis_index("member") * member_rows
    pair_weight = quantity[:, None] * token_area[None, :] / (count * (count - 1))
    for row in range(member_rows):
        magnitude = jnp.zeros_like(own[0])
        pulled = jnp.zeros_like(own[0])
        for other in range(count):
            gap = own[row] - everyone[other]
            square = gap * gap + SMOOTH
            upside = lax.rsqrt(square)
            keep = jnp.where(first + row == other, 0.0, 0.5)
            magnitude = magnitude + keep * square * upside
            pulled = pulled + gap * upside
        share = share - jnp.sum(pair_weight * magnitude)
        slope = slope.at[row].add(-pair_weight * pulled)
    return share, slope


CHUNKS = 8


def reduce_kernel(
    places, product, decoder, out, decoder_out, chunk_slot, member_send, member_recv,
    decoder_send, decoder_recv, first_recv, *rest
):
    groups, bits = places
    sends, recvs = rest[-2:]
    rest = list(rest[:-2])
    me, here = lax.axis_index("token"), lax.axis_index("member")
    low_bits = min(bits, CHUNKS.bit_length() - 1)
    chunks = 1 << low_bits
    width = product.shape[-1]
    half = width // 2
    piece = width // groups
    started = []

    def flip(bit):
        return me + (1 << bit) * (1 - 2 * (lax.div(me, 1 << bit) % 2))

    def bit_of(bit):
        return lax.div(me, 1 << bit) % 2

    def across(low):
        target = me
        for bit in range(low_bits):
            if low >> bit & 1:
                target = target + (1 << bit) * (1 - 2 * bit_of(bit))
        return target

    def send(source, target, device):
        index = len(started)
        copy = pltpu.make_async_remote_copy(
            src_ref=source, dst_ref=target, send_sem=sends.at[index], recv_sem=recvs.at[index],
            device_id=device, device_id_type=pl.DeviceIdType.MESH,
        )
        copy.start()
        started.append(copy)
        return copy

    barrier = pltpu.get_barrier_semaphore()
    token_partners = [across(low) for low in range(1, chunks)]
    token_partners += [flip(bit) for bit in range(low_bits, bits)]
    for partner in token_partners:
        pl.semaphore_signal(
            barrier, inc=1, device_id={"token": partner}, device_id_type=pl.DeviceIdType.MESH
        )
    for ahead in range(1, groups):
        pl.semaphore_signal(
            barrier, inc=1, device_id={"member": lax.rem(here + ahead, groups)},
            device_id_type=pl.DeviceIdType.MESH,
        )
    pl.semaphore_wait(barrier, len(token_partners) + groups - 1)

    copy0 = send(product.at[:, 1 - bit_of(0)], first_recv, {"token": flip(0)})
    lanes = []
    for part, order in enumerate((range(1, bits), range(bits - 1, 0, -1))):
        columns = pl.ds(part * half, half)
        lanes.append(dict(columns=columns, order=list(order), low=part == 0, part=part))
    blocks = 1 << (bits - 1)
    mine0 = bit_of(0)

    dec_send = decoder.at[:, 1 - mine0]
    dec_recv = rest.pop(0)
    dec_copy = send(dec_send, dec_recv, {"token": flip(0)})

    copy0.wait_recv()
    for lane in lanes:
        columns = lane["columns"]
        lane["value"] = lambda q, columns=columns: (
            product[q, mine0, :, columns].astype(jnp.float32)
            + first_recv[q, :, columns].astype(jnp.float32)
        )
    dec_copy.wait_recv()
    decoder_value = lambda q, recv=dec_recv: decoder[q, mine0] + recv[q]

    for step in range(bits - 1):
        blocks //= 2
        for lane in lanes:
            bit = lane["order"][step]
            mine = bit_of(bit)
            place = (
                (lambda q, b: 2 * q + b) if lane["low"] else (lambda q, b, n=blocks: b * n + q)
            )
            send_buf, keep, recv = rest.pop(0), rest.pop(0), rest.pop(0)
            for q in range(blocks):
                send_buf[q] = lane["value"](place(q, 1 - mine)).astype(jnp.bfloat16)
            lane["copy"] = send(send_buf, recv, {"token": flip(bit)})
            for q in range(blocks):
                keep[q] = lane["value"](place(q, mine))
            lane["value"] = lambda q, keep=keep, recv=recv: keep[q] + recv[q].astype(jnp.float32)
        bit = step + 1
        mine = bit_of(bit)
        count = chunks >> (bit + 1) if bit < low_bits else 1
        send_buf, keep, recv = rest.pop(0), rest.pop(0), rest.pop(0)
        if bit < low_bits:
            for q in range(count):
                send_buf[q] = decoder_value(2 * q + 1 - mine)
                keep[q] = decoder_value(2 * q + mine)
        else:
            send_buf[0] = decoder_value(0)
            keep[0] = send_buf[0]
        dec_copy = send(send_buf, recv, {"token": flip(bit)})
        decoder_value = lambda q, keep=keep, recv=recv: keep[q] + recv[q]
        for lane in lanes:
            lane["copy"].wait_recv()
        dec_copy.wait_recv()

    own_total, own_decoder = rest.pop(0), rest.pop(0)
    for lane in lanes:
        total = lane["value"](0)
        for index in range(groups // 2):
            spot = lane["part"] * (groups // 2) + index
            own_total[spot] = total[:, index * piece : (index + 1) * piece]
            member_send[spot] = own_total[spot].astype(jnp.bfloat16)
    total = decoder_value(0)
    for index in range(groups):
        own_decoder[index] = total[:, index * piece : (index + 1) * piece]
    waits = []
    for ahead in range(1, groups):
        target = lax.rem(here + ahead, groups)
        waits.append(send(member_send.at[target], member_recv.at[ahead - 1], {"member": target}))
        waits.append(send(own_decoder.at[target], decoder_recv.at[ahead - 1], {"member": target}))
    for copy in waits:
        copy.wait_recv()
    summed = own_total[here]
    chunk = own_decoder[here]
    for ahead in range(groups - 1):
        summed = summed + member_recv[ahead].astype(jnp.float32)
        chunk = chunk + decoder_recv[ahead]
    gathered = rest.pop(0)
    gathered[here] = summed.astype(jnp.bfloat16)
    decoder_send[here] = chunk
    back, dec_back = [], []
    for ahead in range(1, groups):
        target = lax.rem(here + ahead, groups)
        dec_back.append(send(decoder_send.at[here], decoder_send.at[here], {"member": target}))
        back.append(send(gathered.at[here], gathered.at[here], {"member": target}))
    for copy in dec_back:
        copy.wait_recv()
    mine = lax.rem(me, chunks)
    for index in range(groups):
        chunk_slot[mine, :, index * piece : (index + 1) * piece] = decoder_send[index]
    last = [
        send(chunk_slot.at[mine], chunk_slot.at[mine], {"token": across(low)})
        for low in range(1, chunks)
    ]
    for copy in back:
        copy.wait_recv()
    for index in range(groups):
        out[:, index * piece : (index + 1) * piece] = gathered[index].astype(jnp.float32)
    for copy in last:
        copy.wait_recv()
    decoder_out[...] = chunk_slot[...]
    for copy in started:
        copy.wait_send()


def reduce_gradients(product, decoder):
    count, groups = lax.axis_size("token"), lax.axis_size("member")
    bits = count.bit_length() - 1
    low_bits = min(bits, CHUNKS.bit_length() - 1)
    chunks = 1 << low_bits
    width = product.shape[1]
    rows = product.shape[0] // count
    piece, half = width // groups, width // 2
    deep = -(-decoder.shape[0] // (8 * chunks)) * 8
    padded = jnp.pad(decoder, ((0, deep * chunks - decoder.shape[0]), (0, 0)))
    f32, bf16 = jnp.float32, jnp.bfloat16
    scratch = [
        pltpu.VMEM((chunks, deep, width), f32),
        pltpu.VMEM((groups, rows, piece), bf16),
        pltpu.VMEM((groups - 1, rows, piece), bf16),
        pltpu.VMEM((groups, deep, piece), f32),
        pltpu.VMEM((groups - 1, deep, piece), f32),
        pltpu.VMEM((count // 2, rows, width), bf16),
        pltpu.VMEM((chunks // 2, deep, width), f32),
    ]
    blocks = count // 2
    copies = 2
    for step in range(bits - 1):
        blocks //= 2
        for _ in range(2):
            scratch += [
                pltpu.VMEM((blocks, rows, half), bf16),
                pltpu.VMEM((blocks, rows, half), f32),
                pltpu.VMEM((blocks, rows, half), bf16),
            ]
        left = max(chunks >> (step + 2), 1)
        scratch += [pltpu.VMEM((left, deep, width), f32)] * 3
        copies += 3
    scratch += [
        pltpu.VMEM((groups, rows, piece), f32),
        pltpu.VMEM((groups, deep, piece), f32),
        pltpu.VMEM((groups, rows, piece), bf16),
    ]
    copies += 4 * (groups - 1) + chunks - 1
    scratch += [pltpu.SemaphoreType.DMA((copies,)), pltpu.SemaphoreType.DMA((copies,))]
    out, whole = pl.pallas_call(
        functools.partial(reduce_kernel, (groups, bits)),
        out_shape=(
            jax.ShapeDtypeStruct((rows, width), f32),
            jax.ShapeDtypeStruct((chunks, deep, width), f32),
        ),
        in_specs=[pl.BlockSpec(memory_space=pltpu.VMEM)] * 2,
        out_specs=[pl.BlockSpec(memory_space=pltpu.VMEM)] * 2,
        scratch_shapes=scratch,
        compiler_params=pltpu.CompilerParams(
            collective_id=0, has_side_effects=True, vmem_limit_bytes=40 * 2**20
        ),
    )(
        product.reshape(count // 2, 2, rows, width),
        padded.reshape(chunks // 2, 2, deep, width),
    )
    return out, whole.reshape(chunks * deep, width)


def shards(
    members_in,
    member_noise,
    norm_gain,
    weight_query,
    weight_key,
    weight_value,
    weight_out,
    decoder_projection_weight,
    decoder_bias,
    observations,
    surface_extent_factor,
    quantity_scoring_factor,
    point_map,
):
    member_rows, tokens, width = members_in.shape
    state = members_in.astype(jnp.float32)

    def front(state_in):
        return project(state_in, member_noise, norm_gain, weight_query, weight_key, weight_value)

    (query, key, value), front_pull = jax.vjp(front, state)
    stacked = jnp.stack([key, value])
    below = from_behind(stacked, "token", 1)
    above = from_behind(stacked, "token", -1)
    attended = attention(query, below, stacked, above)
    flat_att = attended.reshape(member_rows * tokens, width)
    update = jnp.dot(flat_att, weight_out, preferred_element_type=jnp.float32).reshape(
        member_rows, tokens, width
    )
    residual_stream_state = (state + member_noise.astype(jnp.float32) + update).astype(jnp.bfloat16)

    own = jnp.einsum(
        "vc,mtc->mvt",
        decoder_projection_weight,
        residual_stream_state,
        preferred_element_type=jnp.float32,
    )
    own = own + decoder_bias[None, :, None]
    share, slope = score_and_slope(
        own, observations, surface_extent_factor, quantity_scoring_factor, point_map
    )
    slope = slope.astype(jnp.bfloat16)
    decoder_piece = jnp.einsum(
        "mvt,mtc->vc", slope, residual_stream_state, preferred_element_type=jnp.float32
    )
    carried_slope = jnp.einsum(
        "mvt,vc->mtc", slope, decoder_projection_weight, preferred_element_type=jnp.float32
    ).astype(jnp.bfloat16)
    flat_grad = carried_slope.reshape(member_rows * tokens, width)
    grad_attended = (
        jnp.dot(flat_grad, weight_out.T, preferred_element_type=jnp.float32)
        .astype(jnp.bfloat16)
        .reshape(member_rows, tokens, width)
    )
    grad_query, lower_rim, inner, upper_rim = attention(
        query, below, stacked, above, grad_attended
    )
    from_next = from_behind(lower_rim, "token", -1)
    from_prev = from_behind(upper_rim, "token", 1)
    inner = inner + from_next.astype(jnp.float32) + from_prev.astype(jnp.float32)
    (grad_front,) = front_pull(
        (grad_query, inner[0].astype(jnp.bfloat16), inner[1].astype(jnp.bfloat16))
    )
    grad_members = (grad_front + carried_slope.astype(jnp.float32)).astype(jnp.bfloat16)
    contract = (((0,), (0,)), ((), ()))
    product = lax.dot_general(flat_att, flat_grad, contract, preferred_element_type=jnp.float32)
    variables = decoder_piece.shape[0]
    decoder_piece = jnp.concatenate([decoder_piece, jnp.full((1, width), share)])
    grad_out, decoder_sum = reduce_gradients(product.astype(jnp.bfloat16), decoder_piece)
    grad_decoder = decoder_sum[:variables]
    mean_scoring = decoder_sum[variables, 0] / (
        observations.shape[0] * observations.shape[1] * lax.axis_size("token")
    )
    return (mean_scoring, grad_members, grad_out, grad_decoder)


def solution(mesh):
    return jax.shard_map(
        shards,
        mesh=mesh,
        in_specs=(
            P("member", "token", None),
            P("member", "token", None),
            P(),
            P(),
            P(),
            P(),
            P(),
            P(),
            P(),
            P(None, "token"),
            P("token"),
            P(),
            P("token"),
        ),
        out_specs=(P(), P("member", "token", None), P("token", None), P()),
        check_vma=False,
    )
```

```python
import functools

import jax
import jax.numpy as jnp
from jax import lax
from jax.experimental import pallas as pl
from jax.experimental.pallas import tpu as pltpu
from jax.sharding import PartitionSpec as P

HEADS = 16
HALF = 128


EPSILON = 1e-06
SMOOTH = 0.01


def from_behind(block, axis, distance):
    devices = range(lax.axis_size(axis))
    route = [(i - distance, i) for i in devices if i - distance in devices]
    return lax.ppermute(block, axis, route)


def head_places(width):
    feature = lax.broadcasted_iota(jnp.int32, (width, HEADS), 0) // (width // HEADS)
    return (feature == lax.broadcasted_iota(jnp.int32, (width, HEADS), 1)).astype(jnp.bfloat16)


def head_mean(flat):
    width = flat.shape[1]
    return split_product(flat, head_places(width), "rc,ch->rh") * (HEADS / width)


def over_heads(each, width):
    return split_product(each, head_places(width), "rh,ch->rc")


@jax.custom_vjp
def normalize_heads(flat):
    return normalize_heads_forward(flat)[0]


def normalize_heads_forward(flat):
    inverse = lax.rsqrt(head_mean(flat * flat) + EPSILON)
    return flat * over_heads(inverse, flat.shape[1]), (flat, inverse)


def normalize_heads_back(saved, slope):
    flat, inverse = saved
    width = flat.shape[1]
    pulled = head_mean(slope * flat) * inverse * inverse * inverse
    return (slope * over_heads(inverse, width) - flat * over_heads(pulled, width),)


normalize_heads.defvjp(normalize_heads_forward, normalize_heads_back)


def project(state_in, member_noise, norm_gain, weight_query, weight_key, weight_value):
    member_rows, tokens, width = state_in.shape
    mixed = state_in + member_noise.astype(jnp.float32)
    normed = (
        mixed * lax.rsqrt(jnp.mean(mixed * mixed, axis=-1, keepdims=True) + EPSILON) * norm_gain
    ).astype(jnp.bfloat16)
    flat = normed.reshape(member_rows * tokens, width)
    query = normalize_heads(jnp.dot(flat, weight_query, preferred_element_type=jnp.float32)).astype(
        jnp.bfloat16
    )
    key = normalize_heads(jnp.dot(flat, weight_key, preferred_element_type=jnp.float32)).astype(
        jnp.bfloat16
    )
    value = jnp.dot(flat, weight_value, preferred_element_type=jnp.float32).astype(jnp.bfloat16)
    full_shape = (member_rows, tokens, width)
    return (query.reshape(full_shape), key.reshape(full_shape), value.reshape(full_shape))


LANES = 256


def lane_pairs(depth):
    lane = lax.broadcasted_iota(jnp.int32, (1, 128), 1)
    return [(lane >= first) & (lane < first + depth) for first in range(0, 128, depth)]


def allowed_keys(tokens):
    index, count = lax.axis_index("token"), lax.axis_size("token")
    row = lax.broadcasted_iota(jnp.int32, (tokens, 3 * tokens), 0)
    column = lax.broadcasted_iota(jnp.int32, (tokens, 3 * tokens), 1)
    least = jnp.where(index == 0, tokens, 0)
    most = jnp.where(index == count - 1, 2 * tokens, 3 * tokens)
    window = (column >= row) & (column < row + 2 * HALF)
    return window & (column >= least) & (column < most)


def product_of(left, right, left_dim, right_dim):
    return lax.dot_general(
        left, right, (((left_dim,), (right_dim,)), ((), ())), preferred_element_type=jnp.float32
    )


def raised_of(query, keys, allowed, scale):
    raised = jnp.where(allowed, jnp.exp(product_of(query, keys, 1, 1) * scale), 0.0)
    return raised / jnp.sum(raised, axis=-1, keepdims=True)


def attend_kernel(depth, query, below, own, above, out):
    tokens = query.shape[1]
    allowed = allowed_keys(tokens)
    scale = depth**-0.5
    for first in range(0, LANES, 128):
        lanes = slice(first, first + 128)
        keys, values = (
            jnp.concatenate([block[kind, 0, :, lanes] for block in (below, own, above)], axis=0)
            for kind in (0, 1)
        )
        mixed = jnp.zeros((tokens, 128), jnp.float32)
        for chosen in lane_pairs(depth):
            picked = jnp.where(chosen, query[0, :, lanes], 0)
            probs = raised_of(picked, keys, allowed, scale).astype(jnp.bfloat16)
            mixed = jnp.where(chosen, product_of(probs, values, 1, 0), mixed)
        out[0, :, lanes] = mixed.astype(jnp.bfloat16)


def attend_back_kernel(
    depth, query, below, own, above, slope, query_out, below_out, own_out, above_out
):
    tokens = query.shape[1]
    allowed = allowed_keys(tokens)
    scale = depth**-0.5
    for first in range(0, LANES, 128):
        lanes = slice(first, first + 128)
        keys, values = (
            jnp.concatenate([block[kind, 0, :, lanes] for block in (below, own, above)], axis=0)
            for kind in (0, 1)
        )
        query_slope = jnp.zeros((tokens, 128), jnp.float32)
        key_slope = jnp.zeros((3 * tokens, 128), jnp.float32)
        value_slope = jnp.zeros((3 * tokens, 128), jnp.float32)
        for chosen in lane_pairs(depth):
            picked = jnp.where(chosen, query[0, :, lanes], 0)
            pulled = jnp.where(chosen, slope[0, :, lanes], 0)
            probs = raised_of(picked, keys, allowed, scale)
            weight = product_of(pulled, values, 1, 1)
            mean = jnp.sum(weight * probs, axis=-1, keepdims=True)
            score_slope = (probs * (weight - mean) * scale).astype(jnp.bfloat16)
            query_slope = jnp.where(chosen, product_of(score_slope, keys, 1, 0), query_slope)
            key_slope = key_slope + product_of(score_slope, picked, 0, 0)
            value_slope = value_slope + product_of(probs.astype(jnp.bfloat16), pulled, 0, 0)
        query_out[0, :, lanes] = query_slope.astype(jnp.bfloat16)
        for kind, total in ((0, key_slope), (1, value_slope)):
            below_out[kind, 0, :, lanes] = total[:tokens].astype(jnp.bfloat16)
            own_out[kind, 0, :, lanes] = total[tokens : 2 * tokens]
            above_out[kind, 0, :, lanes] = total[2 * tokens :].astype(jnp.bfloat16)


def attention(query, below, own, above, slope=None):
    members, tokens, width = query.shape
    assert tokens == HALF
    depth = width // HEADS
    flat = pl.BlockSpec((1, tokens, LANES), lambda m, h: (m, 0, h))
    pair = pl.BlockSpec((2, 1, tokens, LANES), lambda m, h: (0, m, 0, h))
    size = members * tokens * 3 * tokens * width
    half = jax.ShapeDtypeStruct(query.shape, jnp.bfloat16)
    pairs = [
        jax.ShapeDtypeStruct(own.shape, kind) for kind in (jnp.bfloat16, jnp.float32, jnp.bfloat16)
    ]
    if slope is None:
        return pl.pallas_call(
            functools.partial(attend_kernel, depth),
            grid=(members, width // LANES),
            out_shape=half,
            in_specs=[flat, pair, pair, pair],
            out_specs=flat,
            compiler_params=pltpu.CompilerParams(vmem_limit_bytes=24 * 2**20),
            cost_estimate=pl.CostEstimate(
                flops=4 * size, bytes_accessed=16 * query.size, transcendentals=size // depth
            ),
        )(query, below, own, above)
    return pl.pallas_call(
        functools.partial(attend_back_kernel, depth),
        grid=(members, width // LANES),
        out_shape=[half, *pairs],
        in_specs=[flat, pair, pair, pair, flat],
        out_specs=[flat, pair, pair, pair],
        compiler_params=pltpu.CompilerParams(vmem_limit_bytes=24 * 2**20),
        cost_estimate=pl.CostEstimate(
            flops=10 * size, bytes_accessed=36 * query.size, transcendentals=size // depth
        ),
    )(query, below, own, above, slope)


def split_product(left, right, equation):
    high = left.astype(jnp.bfloat16)
    low = (left - high.astype(jnp.float32)).astype(jnp.bfloat16)
    first = jnp.einsum(equation, high, right, preferred_element_type=jnp.float32)
    return first + jnp.einsum(equation, low, right, preferred_element_type=jnp.float32)


def gather_kernel(groups, own, out, slots, sends, recvs):
    here = lax.axis_index("member")
    barrier = pltpu.get_barrier_semaphore()
    for ahead in range(1, groups):
        pl.semaphore_signal(
            barrier, inc=1, device_id={"member": lax.rem(here + ahead, groups)},
            device_id_type=pl.DeviceIdType.MESH,
        )
    pl.semaphore_wait(barrier, groups - 1)
    copies = []
    for ahead in range(1, groups):
        copy = pltpu.make_async_remote_copy(
            src_ref=own, dst_ref=slots.at[here],
            send_sem=sends.at[ahead - 1], recv_sem=recvs.at[ahead - 1],
            device_id={"member": lax.rem(here + ahead, groups)},
            device_id_type=pl.DeviceIdType.MESH,
        )
        copy.start()
        copies.append(copy)
    slots[here] = own[...]
    for copy in copies:
        copy.wait()
    out[...] = slots[...]


def gather_members(own):
    groups = lax.axis_size("member")
    shape = (groups, *own.shape)
    gathered = pl.pallas_call(
        functools.partial(gather_kernel, groups),
        out_shape=jax.ShapeDtypeStruct(shape, own.dtype),
        in_specs=[pl.BlockSpec(memory_space=pltpu.VMEM)],
        out_specs=pl.BlockSpec(memory_space=pltpu.VMEM),
        scratch_shapes=[
            pltpu.VMEM(shape, own.dtype),
            pltpu.SemaphoreType.DMA((groups - 1,)),
            pltpu.SemaphoreType.DMA((groups - 1,)),
        ],
        compiler_params=pltpu.CompilerParams(collective_id=1, has_side_effects=True),
    )(own)
    return gathered.reshape(groups * own.shape[0], *own.shape[1:])


def score_and_slope(own, observed, surface_extent, quantity, point_map):
    member_rows, _, tokens = own.shape
    onehot = point_map[:, None] == lax.iota(jnp.int32, tokens)[None, :]
    token_area = jnp.sum(jnp.where(onehot, surface_extent[:, None], 0.0), axis=0)
    onehot = onehot.astype(jnp.bfloat16)
    everyone = gather_members(own)
    count = everyone.shape[0]
    diff = split_product(own, onehot, "mvt,pt->mvp") - observed[None]
    inverse = lax.rsqrt(diff * diff + SMOOTH)
    weight = quantity[:, None] * surface_extent[None, :] / count
    weighted = weight[None] * inverse
    share = jnp.sum(weighted * (diff * diff + SMOOTH))
    slope = split_product(weighted * diff, onehot, "mvp,pt->mvt")
    first = lax.axis_index("member") * member_rows
    pair_weight = quantity[:, None] * token_area[None, :] / (count * (count - 1))
    for row in range(member_rows):
        magnitude = jnp.zeros_like(own[0])
        pulled = jnp.zeros_like(own[0])
        for other in range(count):
            gap = own[row] - everyone[other]
            square = gap * gap + SMOOTH
            upside = lax.rsqrt(square)
            keep = jnp.where(first + row == other, 0.0, 0.5)
            magnitude = magnitude + keep * square * upside
            pulled = pulled + gap * upside
        share = share - jnp.sum(pair_weight * magnitude)
        slope = slope.at[row].add(-pair_weight * pulled)
    return share, slope


CHUNKS = 8


def reduce_kernel(
    places, product, decoder, out, decoder_out, chunk_slot, member_send, member_recv,
    decoder_send, decoder_recv, first_recv, *rest
):
    groups, bits = places
    sends, recvs = rest[-2:]
    rest = list(rest[:-2])
    me, here = lax.axis_index("token"), lax.axis_index("member")
    low_bits = min(bits, CHUNKS.bit_length() - 1)
    chunks = 1 << low_bits
    width = product.shape[-1]
    half = width // 2
    piece = width // groups
    started = []

    def flip(bit):
        return me + (1 << bit) * (1 - 2 * (lax.div(me, 1 << bit) % 2))

    def bit_of(bit):
        return lax.div(me, 1 << bit) % 2

    def across(low):
        target = me
        for bit in range(low_bits):
            if low >> bit & 1:
                target = target + (1 << bit) * (1 - 2 * bit_of(bit))
        return target

    def send(source, target, device):
        index = len(started)
        copy = pltpu.make_async_remote_copy(
            src_ref=source, dst_ref=target, send_sem=sends.at[index], recv_sem=recvs.at[index],
            device_id=device, device_id_type=pl.DeviceIdType.MESH,
        )
        copy.start()
        started.append(copy)
        return copy

    barrier = pltpu.get_barrier_semaphore()
    token_partners = [across(low) for low in range(1, chunks)]
    token_partners += [flip(bit) for bit in range(low_bits, bits)]
    for partner in token_partners:
        pl.semaphore_signal(
            barrier, inc=1, device_id={"token": partner}, device_id_type=pl.DeviceIdType.MESH
        )
    for ahead in range(1, groups):
        pl.semaphore_signal(
            barrier, inc=1, device_id={"member": lax.rem(here + ahead, groups)},
            device_id_type=pl.DeviceIdType.MESH,
        )
    pl.semaphore_wait(barrier, len(token_partners) + groups - 1)

    copy0 = send(product.at[:, 1 - bit_of(0)], first_recv, {"token": flip(0)})
    lanes = []
    for part, order in enumerate((range(1, bits), range(bits - 1, 0, -1))):
        columns = pl.ds(part * half, half)
        lanes.append(dict(columns=columns, order=list(order), low=part == 0, part=part))
    blocks = 1 << (bits - 1)
    mine0 = bit_of(0)

    dec_send = decoder.at[:, 1 - mine0]
    dec_recv = rest.pop(0)
    dec_copy = send(dec_send, dec_recv, {"token": flip(0)})

    copy0.wait_recv()
    for lane in lanes:
        columns = lane["columns"]
        lane["value"] = lambda q, columns=columns: (
            product[q, mine0, :, columns].astype(jnp.float32)
            + first_recv[q, :, columns].astype(jnp.float32)
        )
    dec_copy.wait_recv()
    decoder_value = lambda q, recv=dec_recv: decoder[q, mine0] + recv[q]

    for step in range(bits - 1):
        blocks //= 2
        for lane in lanes:
            bit = lane["order"][step]
            mine = bit_of(bit)
            place = (
                (lambda q, b: 2 * q + b) if lane["low"] else (lambda q, b, n=blocks: b * n + q)
            )
            send_buf, keep, recv = rest.pop(0), rest.pop(0), rest.pop(0)
            for q in range(blocks):
                send_buf[q] = lane["value"](place(q, 1 - mine)).astype(jnp.bfloat16)
            lane["copy"] = send(send_buf, recv, {"token": flip(bit)})
            for q in range(blocks):
                keep[q] = lane["value"](place(q, mine))
            lane["value"] = lambda q, keep=keep, recv=recv: keep[q] + recv[q].astype(jnp.float32)
        bit = step + 1
        mine = bit_of(bit)
        count = chunks >> (bit + 1) if bit < low_bits else 1
        send_buf, keep, recv = rest.pop(0), rest.pop(0), rest.pop(0)
        if bit < low_bits:
            for q in range(count):
                send_buf[q] = decoder_value(2 * q + 1 - mine)
                keep[q] = decoder_value(2 * q + mine)
        else:
            send_buf[0] = decoder_value(0)
            keep[0] = send_buf[0]
        dec_copy = send(send_buf, recv, {"token": flip(bit)})
        decoder_value = lambda q, keep=keep, recv=recv: keep[q] + recv[q]
        for lane in lanes:
            lane["copy"].wait_recv()
        dec_copy.wait_recv()

    own_total, own_decoder = rest.pop(0), rest.pop(0)
    for lane in lanes:
        total = lane["value"](0)
        for index in range(groups // 2):
            spot = lane["part"] * (groups // 2) + index
            own_total[spot] = total[:, index * piece : (index + 1) * piece]
            member_send[spot] = own_total[spot].astype(jnp.bfloat16)
    total = decoder_value(0)
    for index in range(groups):
        own_decoder[index] = total[:, index * piece : (index + 1) * piece]
    waits = []
    for ahead in range(1, groups):
        target = lax.rem(here + ahead, groups)
        waits.append(send(member_send.at[target], member_recv.at[ahead - 1], {"member": target}))
        waits.append(send(own_decoder.at[target], decoder_recv.at[ahead - 1], {"member": target}))
    for copy in waits:
        copy.wait_recv()
    summed = own_total[here]
    chunk = own_decoder[here]
    for ahead in range(groups - 1):
        summed = summed + member_recv[ahead].astype(jnp.float32)
        chunk = chunk + decoder_recv[ahead]
    gathered = rest.pop(0)
    gathered[here] = summed.astype(jnp.bfloat16)
    decoder_send[here] = chunk
    back, dec_back = [], []
    for ahead in range(1, groups):
        target = lax.rem(here + ahead, groups)
        dec_back.append(send(decoder_send.at[here], decoder_send.at[here], {"member": target}))
        back.append(send(gathered.at[here], gathered.at[here], {"member": target}))
    for copy in dec_back:
        copy.wait_recv()
    mine = lax.rem(me, chunks)
    for index in range(groups):
        chunk_slot[mine, :, index * piece : (index + 1) * piece] = decoder_send[index]
    last = [
        send(chunk_slot.at[mine], chunk_slot.at[mine], {"token": across(low)})
        for low in range(1, chunks)
    ]
    for copy in back:
        copy.wait_recv()
    for index in range(groups):
        out[:, index * piece : (index + 1) * piece] = gathered[index].astype(jnp.float32)
    for copy in last:
        copy.wait_recv()
    decoder_out[...] = chunk_slot[...]
    for copy in started:
        copy.wait_send()


def reduce_gradients(product, decoder):
    count, groups = lax.axis_size("token"), lax.axis_size("member")
    bits = count.bit_length() - 1
    low_bits = min(bits, CHUNKS.bit_length() - 1)
    chunks = 1 << low_bits
    width = product.shape[1]
    rows = product.shape[0] // count
    piece, half = width // groups, width // 2
    deep = -(-decoder.shape[0] // (8 * chunks)) * 8
    padded = jnp.pad(decoder, ((0, deep * chunks - decoder.shape[0]), (0, 0)))
    f32, bf16 = jnp.float32, jnp.bfloat16
    scratch = [
        pltpu.VMEM((chunks, deep, width), f32),
        pltpu.VMEM((groups, rows, piece), bf16),
        pltpu.VMEM((groups - 1, rows, piece), bf16),
        pltpu.VMEM((groups, deep, piece), f32),
        pltpu.VMEM((groups - 1, deep, piece), f32),
        pltpu.VMEM((count // 2, rows, width), bf16),
        pltpu.VMEM((chunks // 2, deep, width), f32),
    ]
    blocks = count // 2
    copies = 2
    for step in range(bits - 1):
        blocks //= 2
        for _ in range(2):
            scratch += [
                pltpu.VMEM((blocks, rows, half), bf16),
                pltpu.VMEM((blocks, rows, half), f32),
                pltpu.VMEM((blocks, rows, half), bf16),
            ]
        left = max(chunks >> (step + 2), 1)
        scratch += [pltpu.VMEM((left, deep, width), f32)] * 3
        copies += 3
    scratch += [
        pltpu.VMEM((groups, rows, piece), f32),
        pltpu.VMEM((groups, deep, piece), f32),
        pltpu.VMEM((groups, rows, piece), bf16),
    ]
    copies += 4 * (groups - 1) + chunks - 1
    scratch += [pltpu.SemaphoreType.DMA((copies,)), pltpu.SemaphoreType.DMA((copies,))]
    out, whole = pl.pallas_call(
        functools.partial(reduce_kernel, (groups, bits)),
        out_shape=(
            jax.ShapeDtypeStruct((rows, width), f32),
            jax.ShapeDtypeStruct((chunks, deep, width), f32),
        ),
        in_specs=[pl.BlockSpec(memory_space=pltpu.VMEM)] * 2,
        out_specs=[pl.BlockSpec(memory_space=pltpu.VMEM)] * 2,
        scratch_shapes=scratch,
        compiler_params=pltpu.CompilerParams(
            collective_id=0, has_side_effects=True, vmem_limit_bytes=40 * 2**20
        ),
        cost_estimate=pl.CostEstimate(
            flops=4 * 10**10, bytes_accessed=4 * product.size, transcendentals=0
        ),
    )(
        product.reshape(count // 2, 2, rows, width),
        padded.reshape(chunks // 2, 2, deep, width),
    )
    return out, whole.reshape(chunks * deep, width)


def shards(
    members_in,
    member_noise,
    norm_gain,
    weight_query,
    weight_key,
    weight_value,
    weight_out,
    decoder_projection_weight,
    decoder_bias,
    observations,
    surface_extent_factor,
    quantity_scoring_factor,
    point_map,
):
    member_rows, tokens, width = members_in.shape
    state = members_in.astype(jnp.float32)

    def front(state_in):
        return project(state_in, member_noise, norm_gain, weight_query, weight_key, weight_value)

    (query, key, value), front_pull = jax.vjp(front, state)
    stacked = jnp.stack([key, value])
    below = from_behind(stacked, "token", 1)
    above = from_behind(stacked, "token", -1)
    attended = attention(query, below, stacked, above)
    flat_att = attended.reshape(member_rows * tokens, width)
    update = jnp.dot(flat_att, weight_out, preferred_element_type=jnp.float32).reshape(
        member_rows, tokens, width
    )
    residual_stream_state = (state + member_noise.astype(jnp.float32) + update).astype(jnp.bfloat16)

    own = jnp.einsum(
        "vc,mtc->mvt",
        decoder_projection_weight,
        residual_stream_state,
        preferred_element_type=jnp.float32,
    )
    own = own + decoder_bias[None, :, None]
    share, slope = score_and_slope(
        own, observations, surface_extent_factor, quantity_scoring_factor, point_map
    )
    slope = slope.astype(jnp.bfloat16)
    decoder_piece = jnp.einsum(
        "mvt,mtc->vc", slope, residual_stream_state, preferred_element_type=jnp.float32
    )
    carried_slope = jnp.einsum(
        "mvt,vc->mtc", slope, decoder_projection_weight, preferred_element_type=jnp.float32
    ).astype(jnp.bfloat16)
    flat_grad = carried_slope.reshape(member_rows * tokens, width)
    grad_attended = (
        jnp.dot(flat_grad, weight_out.T, preferred_element_type=jnp.float32)
        .astype(jnp.bfloat16)
        .reshape(member_rows, tokens, width)
    )
    grad_query, lower_rim, inner, upper_rim = attention(
        query, below, stacked, above, grad_attended
    )
    from_next = from_behind(lower_rim, "token", -1)
    from_prev = from_behind(upper_rim, "token", 1)
    inner = inner + from_next.astype(jnp.float32) + from_prev.astype(jnp.float32)
    contract = (((0,), (0,)), ((), ()))
    product = lax.dot_general(flat_att, flat_grad, contract, preferred_element_type=jnp.float32)
    variables = decoder_piece.shape[0]
    product, decoder_piece, grad_query = lax.optimization_barrier(
        (product, decoder_piece, grad_query)
    )
    decoder_piece = jnp.concatenate([decoder_piece, jnp.full((1, width), share)])
    grad_out, decoder_sum = reduce_gradients(product.astype(jnp.bfloat16), decoder_piece)
    grad_decoder = decoder_sum[:variables]
    mean_scoring = decoder_sum[variables, 0] / (
        observations.shape[0] * observations.shape[1] * lax.axis_size("token")
    )
    (grad_front,) = front_pull(
        (grad_query, inner[0].astype(jnp.bfloat16), inner[1].astype(jnp.bfloat16))
    )
    grad_members = (grad_front + carried_slope.astype(jnp.float32)).astype(jnp.bfloat16)
    return (mean_scoring, grad_members, grad_out, grad_decoder)


def solution(mesh):
    return jax.shard_map(
        shards,
        mesh=mesh,
        in_specs=(
            P("member", "token", None),
            P("member", "token", None),
            P(),
            P(),
            P(),
            P(),
            P(),
            P(),
            P(),
            P(None, "token"),
            P("token"),
            P(),
            P("token"),
        ),
        out_specs=(P(), P("member", "token", None), P("token", None), P()),
        check_vma=False,
    )
```
